128 devices in a mesh: batch: 32 (over z, x_lo, y), tensor: 4 (over x_hi, core).
Axes of the slice: x: 4 (x_hi: 2, x_lo: 2; x = x_hi * 2 + x_lo), y: 4, z: 4, core: 2. Of those that a mesh axis runs over, the one named last changes fastest.
Arguments:
- target_latents: bfloat16 [8192, 2048], P('batch', 'tensor'), may hold values from -6 to 6
- walk_noise: bfloat16 [4, 8192, 2048], P(None, 'batch', 'tensor'), may hold values from -6 to 6
- step_sizes: float32 [4], replicated, may hold values from 0.05 to 0.2
- back_gain: float32 [2048], replicated, may hold values from 0.1 to 1.9
- back_expand: bfloat16 [2048, 4096], P(None, 'tensor'), may hold values from -0.125 to 0.125
- back_clock: float32 [4096], P('tensor'), may hold values from -4 to 4
- back_reduce: bfloat16 [4096, 2048], P('tensor'), may hold values from -0.09375 to 0.09375
- bridge_times: float32 [8192], P('batch'), may hold values from 0.05 to 0.9
- bridge_noise: bfloat16 [8192, 2048], P('batch', 'tensor'), may hold values from -6 to 6
- fore_gain: float32 [2048], replicated, may hold values from 0.1 to 1.9
- fore_expand: bfloat16 [2048, 4096], P(None, 'tensor'), may hold values from -0.125 to 0.125
- fore_clock: float32 [4096], P('tensor'), may hold values from -4 to 4
- fore_reduce: bfloat16 [4096, 2048], P('tensor'), may hold values from -0.09375 to 0.09375
Outputs:
- walk_end: float32 [8192, 2048], P('batch', 'tensor')
- grad_expand: float32 [2048, 4096], P('batch', 'tensor')
- grad_reduce_t: float32 [2048, 4096], P('batch', 'tensor')
The draws below stay inside these ranges and needn't reach their ends.
All inputs are finite; a program needn't handle non-finite values.
Results may differ from the reference program's by a relative error of at most 0.0055.
Values may be sent and summed in bfloat16 or wider, within the bound.
A program may use at most 128 MiB of HBM per device.

```python
import math
import jax
import jax.numpy as jnp
from jax import lax

D = 2048
FF = 4096
STEPS = 4
TOK_DEV = 256
TOKENS = 8192
N_BATCH = 32


def raised(values, stream_key, source, target, parts, factor):
    owner, partner = [(jnp.arange(values.shape[axis_at]) // (values.shape[axis_at] // parts)).reshape([-1 if axis == axis_at else 1 for axis in range(values.ndim)]) for axis_at in (source, target)]
    chosen = jax.random.permutation(stream_key, parts)[partner]
    strong = (owner == chosen) | (owner == (partner + parts // 2) % parts)
    return jnp.where(strong, factor * values, values)


def shard_levels(stream_key, extent, split, smallest, largest):
    factor_of, own = 1.0, jax.random.fold_in(stream_key, 6)
    for dim, parts in split:
        steps = jnp.exp(jax.random.uniform(jax.random.fold_in(own, dim), (parts,), jnp.float32, smallest / len(split), largest / len(split)))
        factor_of = factor_of * jnp.repeat(steps, extent[dim] // parts).reshape([-1 if axis == dim else 1 for axis in range(len(extent))])
    return factor_of


def centred(key, dims, spread, most, cuts=(), kind=jnp.bfloat16):
    level = shard_levels(key, dims, cuts, -0.22, 0.18) if cuts else 1.0
    result = jax.random.normal(key, dims, jnp.float32) * spread * level
    return jnp.minimum(jnp.maximum(result, -most), most).astype(kind)


def noise_with(key, shape, scale, reach, split, heavy, dtype=jnp.bfloat16):
    values = scale * jax.random.normal(key, shape, jnp.float32)
    if split:
        values = values * shard_levels(key, shape, split, -0.22, 0.18)
    return jnp.clip(raised(values, jax.random.fold_in(key, 3), *heavy), -reach, reach).astype(dtype)


def setup_inputs(seed: int = 0) -> dict:
    keys = jax.random.split(jax.random.key(seed), 14)
    target_latents = centred(keys[0], (TOKENS, D), 1.0, 6.0, ((0, 32), (1, 4)))
    walk_noise = centred(keys[1], (STEPS, TOKENS, D), 1.0, 6.0, ((1, 32), (2, 4)))
    step_sizes = jnp.clip(jnp.exp(jax.random.uniform(keys[2], (STEPS,), jnp.float32, math.log(0.05), math.log(0.2))), 0.05, 0.2)
    back_gain = jnp.clip(1.0 + 0.18 * jax.random.normal(keys[3], (D,), jnp.float32), 0.1, 1.9)
    back_expand = centred(keys[4], (D, FF), D ** -0.5, 0.125, ((1, 4),))
    back_clock = centred(keys[5], (FF,), 1.0, 4.0, ((0, 4),), jnp.float32)
    back_reduce = centred(keys[6], (FF, D), FF ** -0.5, 0.09375, ((0, 4),))
    bridge_times = jnp.clip(0.05 + 0.84999998 * jax.random.uniform(keys[7], (TOKENS,), jnp.float32) ** shard_levels(keys[7], (TOKENS,), ((0, 32),), -0.2, 0.2), 0.05, 0.9)
    bridge_noise = noise_with(keys[8], (TOKENS, D), 1.0, 6.0, ((0, 32), (1, 4)), (0, 1, 32, 2.75))
    fore_gain = jnp.clip(1.0 + 0.18 * jax.random.normal(keys[9], (D,), jnp.float32), 0.1, 1.9)
    fore_expand = centred(keys[10], (D, FF), D ** -0.5, 0.125, ((1, 4),))
    fore_clock = centred(keys[11], (FF,), 1.0, 4.0, ((0, 4),), jnp.float32)
    fore_reduce = centred(keys[12], (FF, D), FF ** -0.5, 0.09375, ((0, 4),))
    return dict(target_latents=target_latents, walk_noise=walk_noise, step_sizes=step_sizes, back_gain=back_gain, back_expand=back_expand, back_clock=back_clock, back_reduce=back_reduce, bridge_times=bridge_times, bridge_noise=bridge_noise, fore_gain=fore_gain, fore_expand=fore_expand, fore_clock=fore_clock, fore_reduce=fore_reduce)


NOISE_LEVEL = 0.5
EPSILON = 1e-06

def normalize(rows, gain):
    float_rows = rows.astype(jnp.float32)
    factor = lax.rsqrt(lax.optimization_barrier(jnp.mean(float_rows * float_rows, axis=1, keepdims=True)) + EPSILON)
    return (float_rows * factor * gain).astype(jnp.bfloat16)

def regroup(array):
    pieces = array.reshape(N_BATCH, N_BATCH, TOK_DEV // N_BATCH, D)
    return jnp.swapaxes(pieces, 0, 1).reshape(TOKENS, D)

def reference(target_latents, walk_noise, step_sizes, back_gain, back_expand, back_clock, back_reduce, bridge_times, bridge_noise, fore_gain, fore_expand, fore_clock, fore_reduce):
    walk_state = target_latents.astype(jnp.float32)
    walk_clock = jnp.float32(1.0)
    for step_index in range(STEPS):
        normed = normalize(walk_state.astype(jnp.bfloat16), back_gain)
        hidden = jnp.dot(normed, back_expand, preferred_element_type=jnp.float32) + walk_clock * back_clock
        active = jax.nn.silu(hidden).astype(jnp.bfloat16)
        drift = jnp.dot(active, back_reduce, preferred_element_type=jnp.float32)
        step_width = step_sizes[step_index]
        walk_state = walk_state - step_width * drift + jnp.sqrt(step_width) * NOISE_LEVEL * walk_noise[step_index].astype(jnp.float32)
        walk_clock = walk_clock - step_width
    walk_end = walk_state
    start_float = regroup(walk_end.astype(jnp.bfloat16)).astype(jnp.float32)
    end_float = regroup(target_latents).astype(jnp.float32)
    bridge_tau = bridge_times[:, None]
    interpolant = (1.0 - bridge_tau) * start_float + bridge_tau * end_float + jnp.sqrt(bridge_tau * (1.0 - bridge_tau)) * NOISE_LEVEL * bridge_noise.astype(jnp.float32)
    target_flow = (end_float - interpolant) / (1.0 - bridge_tau)
    normed = normalize(interpolant.astype(jnp.bfloat16), fore_gain)
    hidden = jnp.dot(normed, fore_expand, preferred_element_type=jnp.float32) + bridge_tau * fore_clock
    active = jax.nn.silu(hidden).astype(jnp.bfloat16)
    predicted = jnp.dot(active, fore_reduce, preferred_element_type=jnp.float32)
    loss_scale = 1.0 / jnp.sqrt(jnp.float32(TOKENS))
    scaled_error = ((predicted - target_flow) * loss_scale).astype(jnp.bfloat16)
    back_hidden = lax.dot_general(scaled_error, fore_reduce, (((1,), (1,)), ((), ())), preferred_element_type=jnp.float32)
    sigmoid_part = jax.nn.sigmoid(hidden)
    silu_slope = sigmoid_part * (1.0 + hidden * (1.0 - sigmoid_part))
    hidden_grad = (back_hidden * silu_slope).astype(jnp.bfloat16)
    grad_expand = lax.dot_general(normed, hidden_grad, (((0,), (0,)), ((), ())), preferred_element_type=jnp.float32)
    grad_reduce_t = lax.dot_general(scaled_error, active, (((0,), (0,)), ((), ())), preferred_element_type=jnp.float32)
    return (walk_end, grad_expand, grad_reduce_t)
```

```python
import jax
import jax.numpy as jnp
from jax import lax
from jax.experimental import pallas as pl
from jax.experimental.pallas import tpu as pltpu
from jax.sharding import PartitionSpec as P

NOISE_LEVEL = 0.5
EPSILON = 1e-06
MESH = pl.DeviceIdType.MESH
F32 = jnp.float32
BF16 = jnp.bfloat16
STREAMS = 2
ROWS = 128


def place():
    b = lax.axis_index("batch")
    t = lax.axis_index("tensor")
    return b // 8, (b // 4) % 2, b % 4, t // 2, t % 2


def device(z, l, y, h, c):
    return (z * 8 + l * 4 + y, h * 2 + c)


def remote(src, dst, send_sem, recv_sem, dev):
    return pltpu.make_async_remote_copy(
        src_ref=src, dst_ref=dst, send_sem=send_sem, recv_sem=recv_sem, device_id=dev, device_id_type=MESH
    )


def greet(devices):
    barrier = pltpu.get_barrier_semaphore()
    for dev in devices:
        pl.semaphore_signal(barrier, inc=1, device_id=dev, device_id_type=MESH)
    return lambda: pl.semaphore_wait(barrier, len(devices))


def batch_peers(z, l, y, h, c):
    peers = [device(z, 1 - l, y, h, c)]
    peers += [device(z, l, (y + d) % 4, h, c) for d in (1, 2, 3)]
    peers += [device((z + d) % 4, l, y, h, c) for d in (1, 2, 3)]
    return peers


def net_kernel(
    x_ref, wn_hbm, steps_ref, bg_ref, be_hbm, bc_ref, br_hbm, bt_ref, bn_ref, fg_ref, fe_hbm, fc_ref, fr_hbm,
    walk_ref, normed_ref, err_ref, hg_ref, act_ref,
    be, br, fe, fr, wn, u, nb, ab, pcs, pcr, pfs, pfr, own, flow, hid, tau, m0, m1, m2, m3,
    load_sem, ss, rs, ms, mr,
):
    z, l, y, h, c = place()
    core_dev = device(z, l, y, h, 1 - c)
    far_dev = device(z, l, y, 1 - h, c)
    q_own, q_far = 2 * h + c, 2 * (1 - h) + c

    loads = [
        pltpu.make_async_copy(src, dst, load_sem.at[i])
        for i, (src, dst) in enumerate(((be_hbm, be), (br_hbm, br), (wn_hbm, wn), (fe_hbm, fe), (fr_hbm, fr)))
    ]
    for load in loads:
        load.start()
    arrived = greet([core_dev, far_dev] + batch_peers(z, l, y, h, c))

    def rows(s):
        return slice(s * ROWS, (s + 1) * ROWS)

    def ag_core(s):
        return remote(u.at[s, q_own], u.at[s, q_own], ss.at[0, s], rs.at[0, s], core_dev)

    def ag_far(s):
        return remote(u.at[s, q_own], u.at[s, q_own], ss.at[1, s], rs.at[1, s], far_dev)

    def ag_fwd(s):
        return remote(u.at[s, q_far], u.at[s, q_far], ss.at[2, s], rs.at[2, s], core_dev)

    def rs_core(s, i):
        side = (1 - h) if i == 0 else h
        return remote(pcs.at[s, side], pcr.at[s, side], ss.at[3 + i, s], rs.at[3 + i, s], core_dev)

    def rs_far(s):
        return remote(pfs.at[s], pfr.at[s], ss.at[5, s], rs.at[5, s], far_dev)

    def gather_start(s):
        ag_far(s).start()
        ag_core(s).start()

    def gather_wait(s):
        ag_far(s).wait_recv()
        ag_fwd(s).start()
        ag_core(s).wait_recv()
        ag_fwd(s).wait_recv()

    def put_own(s, value):
        ag_core(s).wait_send()
        ag_far(s).wait_send()
        u[s, q_own] = value.astype(BF16)

    def normalize(s, gain_ref):
        parts = [u[s, q].astype(F32) for q in range(4)]
        total = sum(jnp.sum(p * p, axis=1, keepdims=True) for p in parts)
        factor = lax.rsqrt(total * (1.0 / 2048.0) + EPSILON)
        for q in range(4):
            nb[:, 512 * q : 512 * (q + 1)] = (parts[q] * factor * gain_ref[:, 512 * q : 512 * (q + 1)]).astype(BF16)

    def reduce_start(s, active, reduce_ref):
        for i in range(2):
            side = (1 - h) if i == 0 else h
            column = pl.multiple_of((2 * side + 1 - c) * 512, 512)
            pcs[s, side] = jnp.dot(active, reduce_ref[:, pl.ds(column, 512)], preferred_element_type=F32)
            rs_core(s, i).start()
        part = jnp.dot(
            active, reduce_ref[:, pl.ds(pl.multiple_of(q_far * 512, 512), 512)], preferred_element_type=F32
        )
        rs_core(s, 0).wait_recv()
        ag_fwd(s).wait_send()
        pfs[s] = (part + pcr[s, 1 - h]).astype(BF16)
        rs_far(s).start()
        part = jnp.dot(
            active, reduce_ref[:, pl.ds(pl.multiple_of(q_own * 512, 512), 512)], preferred_element_type=F32
        )
        rs_core(s, 1).wait_recv()
        own[s] = part + pcr[s, h]
        rs_core(s, 0).wait_send()
        rs_core(s, 1).wait_send()

    def reduce_wait(s):
        rs_far(s).wait()
        return own[s] + pfr[s].astype(F32)

    for s in range(STREAMS):
        u[s, q_own] = x_ref[rows(s)]
        walk_ref[rows(s)] = x_ref[rows(s)].astype(F32)
    arrived()
    for s in range(STREAMS):
        gather_start(s)

    for s in range(STREAMS):
        noise = bn_ref[rows(s)].astype(F32).reshape(16, 8, 512)
        times = jnp.transpose(jnp.broadcast_to(bt_ref[s : s + 1, :], (128, 128)))
        high = times.astype(BF16).astype(F32)
        low = times - high
        packed = jnp.concatenate([noise[:, :, :256], noise[:, :, 256:]], axis=1)
        clocks = jnp.concatenate([high.reshape(16, 8, 128), low.reshape(16, 8, 128)], axis=1)
        m0[2 * s : 2 * s + 2] = (
            jnp.concatenate([packed, clocks], axis=2).astype(BF16).reshape(2, 2, 4, 16, 384)
        )

    def swap_l():
        return remote(m0.at[:, 1 - l], m1.at[:, l], ms.at[0], mr.at[0], device(z, 1 - l, y, h, c))

    def swap_y(d):
        to = (y + d) % 4
        return remote(m1.at[:, :, to], m2.at[:, :, y], ms.at[d], mr.at[d], device(z, l, to, h, c))

    def swap_z(d):
        to = (z + d) % 4
        return remote(m2.at[to], m3.at[z], ms.at[3 + d], mr.at[3 + d], device(to, l, y, h, c))

    swap_l().start()
    m1[:, l] = m0[:, l]

    loads[0].wait()
    loads[1].wait()
    loads[2].wait()

    def step(k, clock):
        width = steps_ref[k]
        for s in range(STREAMS):
            gather_wait(s)
            normalize(s, bg_ref)
            for n in range(4):
                cols = slice(256 * n, 256 * (n + 1))
                hidden = jnp.dot(nb[...], be[:, cols], preferred_element_type=F32) + clock * bc_ref[:, cols]
                ab[:, cols] = (hidden * jax.nn.sigmoid(hidden)).astype(BF16)
            reduce_start(s, ab[...], br)

        @pl.when(k == 0)
        def _():
            swap_l().wait()
            for d in (1, 2, 3):
                swap_y(d).start()
            m2[:, :, y] = m1[:, :, y]

        @pl.when(k == 1)
        def _():
            for d in (1, 2, 3):
                swap_y(d).wait()
            for d in (1, 2, 3):
                swap_z(d).start()
            m3[z] = m2[z]

        @pl.when(k == 3)
        def _():
            for d in (1, 2, 3):
                swap_z(d).wait()

        spread = jnp.sqrt(jnp.full((1, 512), width, F32)) * NOISE_LEVEL
        for s in range(STREAMS):
            drift = reduce_wait(s)
            state = walk_ref[rows(s)] - width * drift + spread * wn[k, rows(s)].astype(F32)
            walk_ref[rows(s)] = state

            @pl.when(k < 3)
            def _():
                put_own(s, state)

            @pl.when(k == 3)
            def _():
                message = m3[2 * s : 2 * s + 2].reshape(16, 16, 384).astype(F32)
                noise = jnp.concatenate(
                    [message[:, :8, :256].reshape(ROWS, 256), message[:, 8:, :256].reshape(ROWS, 256)], axis=1
                )
                times = (message[:, :8, 256:] + message[:, 8:, 256:]).reshape(ROWS, 128)
                tau[s] = times
                times = jnp.concatenate([times] * 4, axis=1)
                start = state.astype(BF16).astype(F32)
                end = x_ref[rows(s)].astype(F32)
                mixed = (1.0 - times) * start + times * end + jnp.sqrt(times * (1.0 - times)) * NOISE_LEVEL * noise
                flow[s] = (end - mixed) / (1.0 - times)
                put_own(s, mixed)

            gather_start(s)
        return clock - width

    lax.fori_loop(0, 4, step, jnp.float32(1.0))

    loads[3].wait()
    loads[4].wait()
    for s in range(STREAMS):
        gather_wait(s)
        normalize(s, fg_ref)
        normed_ref[rows(s)] = nb[...]
        times = jnp.concatenate([tau[s]] * 2, axis=1)
        for n in range(4):
            cols = slice(256 * n, 256 * (n + 1))
            hidden = jnp.dot(nb[...], fe[:, cols], preferred_element_type=F32) + times * fc_ref[:, cols]
            hid[s, :, cols] = hidden
            act_ref[rows(s), cols] = (hidden * jax.nn.sigmoid(hidden)).astype(BF16)
        reduce_start(s, act_ref[rows(s)], fr)
    scale = 1.0 / (8192.0**0.5)
    for s in range(STREAMS):
        put_own(s, (reduce_wait(s) - flow[s]) * scale)
        gather_start(s)
    for s in range(STREAMS):
        gather_wait(s)
        for q in range(4):
            err_ref[rows(s), 512 * q : 512 * (q + 1)] = u[s, q]
        for n in range(4):
            cols = slice(256 * n, 256 * (n + 1))
            back = lax.dot_general(
                err_ref[rows(s)], fr[cols, :], (((1,), (1,)), ((), ())), preferred_element_type=F32
            )
            hidden = hid[s, :, cols]
            sig = jax.nn.sigmoid(hidden)
            hg_ref[rows(s), cols] = (back * (sig * (1.0 + hidden * (1.0 - sig)))).astype(BF16)
    for s in range(STREAMS):
        ag_core(s).wait_send()
        ag_far(s).wait_send()
        ag_fwd(s).wait_send()


def grad_kernel(
    normed_ref, err_ref, hg_ref, act_ref, ge_ref, gr_ref, g0, g1, r1, a0, a1, r2, b, r3, ss, rs
):
    z, l, y, h, c = place()
    arrived = greet(batch_peers(z, l, y, h, c))

    def ydev(d):
        return device(z, l, (y + d) % 4, h, c)

    def zdev(d):
        return device((z + d) % 4, l, y, h, c)

    def first(p, d, chunk):
        if p == 0:
            to = (y + d) % 4
            return remote(g0.at[chunk, to], r1.at[0, d - 1, chunk], ss.at[0, d - 1], rs.at[0, d - 1], ydev(d))
        to = (z + d) % 4
        return remote(
            g1.at[to, chunk], r1.at[1, d - 1, chunk], ss.at[1, d - 1], rs.at[1, d - 1], zdev(d)
        )

    def first_all(p, d):
        if p == 0:
            return remote(g0.at[:, (y + d) % 4], r1.at[0, d - 1], ss.at[0, d - 1], rs.at[0, d - 1], ydev(d))
        return remote(g1.at[(z + d) % 4], r1.at[1, d - 1], ss.at[1, d - 1], rs.at[1, d - 1], zdev(d))

    def second(p, d):
        if p == 0:
            return remote(a0.at[(z + d) % 4], r2.at[0, d - 1], ss.at[2, d - 1], rs.at[2, d - 1], zdev(d))
        return remote(a1.at[:, (y + d) % 4], r2.at[1, d - 1], ss.at[3, d - 1], rs.at[3, d - 1], ydev(d))

    def third(p):
        return remote(b.at[p, 1 - l], r3.at[p], ss.at[4, p], rs.at[4, p], device(z, 1 - l, y, h, c))

    arrived()

    def make0(i, _):
        left = err_ref[:, pl.ds(pl.multiple_of(i * 256, 256), 256)]
        part = lax.dot_general(left, act_ref[...], (((0,), (0,)), ((), ())), preferred_element_type=F32)
        g0[i] = part.astype(BF16).reshape(4, 64, 1024)
        for d in (1, 2, 3):
            first(0, d, i).start()
        return 0

    lax.fori_loop(0, 8, make0, 0)

    def make1(j, _):
        to = (z + 1 + j // 2) % 4
        half = j % 2
        left = normed_ref[:, pl.ds(pl.multiple_of((to * 2 + half) * 256, 256), 256)]
        part = lax.dot_general(left, hg_ref[...], (((0,), (0,)), ((), ())), preferred_element_type=F32)
        g1[to, pl.ds(half * 4, 4)] = part.astype(BF16).reshape(4, 64, 1024)
        return 0

    for d in (1, 2, 3):
        lax.fori_loop(2 * d - 2, 2 * d, make1, 0)
        first_all(1, d).start()
    lax.fori_loop(6, 8, make1, 0)

    for p in (0, 1):
        for d in (1, 2, 3):
            first_all(p, d).wait()

        def add1(i, _):
            mine = g0[i, y] if p == 0 else g1[z, i]
            total = mine.astype(F32) + sum(r1[p, d, i].astype(F32) for d in range(3))
            if p == 0:
                a0[i // 2, i % 2] = total.astype(BF16)
            else:
                a1[i // 4, i % 4] = total.astype(BF16)
            return 0

        lax.fori_loop(0, 8, add1, 0)
        for d in (1, 2, 3):
            second(p, d).start()
    for p in (0, 1):
        for d in (1, 2, 3):
            second(p, d).wait()
        for i in range(2):
            mine = a0[z, i] if p == 0 else a1[i, y]
            b[p, i] = mine.astype(F32) + sum(r2[p, d, i].astype(F32) for d in range(3))
        third(p).start()
    for p, out in ((0, gr_ref), (1, ge_ref)):
        third(p).wait()
        out[...] = b[p, l] + r3[p]


def body(
    target_latents, walk_noise, step_sizes, back_gain, back_expand, back_clock, back_reduce,
    bridge_times, bridge_noise, fore_gain, fore_expand, fore_clock, fore_reduce,
):
    vmem = pl.BlockSpec(memory_space=pltpu.VMEM)
    smem = pl.BlockSpec(memory_space=pltpu.SMEM)
    hbm = pl.BlockSpec(memory_space=pl.ANY)
    dma = pltpu.SemaphoreType.DMA
    sds = jax.ShapeDtypeStruct
    S, R = STREAMS, ROWS
    walk_end, normed, err, hg, act = pl.pallas_call(
        net_kernel,
        out_shape=(
            sds((256, 512), F32), sds((256, 2048), BF16), sds((256, 2048), BF16),
            sds((256, 1024), BF16), sds((256, 1024), BF16),
        ),
        in_specs=[vmem, hbm, smem, vmem, hbm, vmem, hbm, vmem, vmem, vmem, hbm, vmem, hbm],
        out_specs=(vmem,) * 5,
        scratch_shapes=[
            pltpu.VMEM((2048, 1024), BF16), pltpu.VMEM((1024, 2048), BF16),
            pltpu.VMEM((2048, 1024), BF16), pltpu.VMEM((1024, 2048), BF16),
            pltpu.VMEM((4, 256, 512), BF16),
            pltpu.VMEM((S, 4, R, 512), BF16),
            pltpu.VMEM((R, 2048), BF16), pltpu.VMEM((R, 1024), BF16),
            pltpu.VMEM((S, 2, R, 512), F32), pltpu.VMEM((S, 2, R, 512), F32),
            pltpu.VMEM((S, R, 512), BF16), pltpu.VMEM((S, R, 512), BF16),
            pltpu.VMEM((S, R, 512), F32), pltpu.VMEM((S, R, 512), F32),
            pltpu.VMEM((S, R, 1024), F32), pltpu.VMEM((S, R, 128), F32),
        ]
        + [pltpu.VMEM((4, 2, 4, 16, 384), BF16)] * 4
        + [dma((5,)), dma((6, S)), dma((6, S)), dma((7,)), dma((7,))],
        compiler_params=pltpu.CompilerParams(
            collective_id=0, has_side_effects=True, vmem_limit_bytes=56 * 2**20
        ),
        name="net",
    )(
        target_latents, walk_noise, step_sizes, back_gain.reshape(1, 2048), back_expand,
        back_clock.reshape(1, 1024), back_reduce, bridge_times.reshape(2, 128), bridge_noise,
        fore_gain.reshape(1, 2048), fore_expand, fore_clock.reshape(1, 1024), fore_reduce,
    )
    grad_expand, grad_reduce_t = pl.pallas_call(
        grad_kernel,
        out_shape=(sds((64, 1024), F32), sds((64, 1024), F32)),
        in_specs=[vmem] * 4,
        out_specs=(vmem, vmem),
        scratch_shapes=[
            pltpu.VMEM((8, 4, 64, 1024), BF16), pltpu.VMEM((4, 8, 64, 1024), BF16),
            pltpu.VMEM((2, 3, 8, 64, 1024), BF16),
            pltpu.VMEM((4, 2, 64, 1024), BF16), pltpu.VMEM((2, 4, 64, 1024), BF16),
            pltpu.VMEM((2, 3, 2, 64, 1024), BF16),
            pltpu.VMEM((2, 2, 64, 1024), F32), pltpu.VMEM((2, 64, 1024), F32),
            dma((5, 3)), dma((5, 3)),
        ],
        compiler_params=pltpu.CompilerParams(
            collective_id=1, has_side_effects=True, vmem_limit_bytes=56 * 2**20
        ),
        name="grad",
    )(normed, err, hg, act)
    return walk_end, grad_expand, grad_reduce_t


def solution(mesh):
    placed = (
        P("batch", "tensor"), P(None, "batch", "tensor"), P(), P(), P(None, "tensor"), P("tensor"),
        P("tensor", None), P("batch"), P("batch", "tensor"), P(), P(None, "tensor"), P("tensor"),
        P("tensor", None),
    )
    return jax.shard_map(
        body, mesh=mesh, in_specs=placed,
        out_specs=(P("batch", "tensor"), P("batch", "tensor"), P("batch", "tensor")), check_vma=False,
    )
```

```python
import jax
import jax.numpy as jnp
from jax import lax
from jax.experimental import pallas as pl
from jax.experimental.pallas import tpu as pltpu
from jax.sharding import PartitionSpec as P

NOISE_LEVEL = 0.5
EPSILON = 1e-06
MESH = pl.DeviceIdType.MESH
F32 = jnp.float32
BF16 = jnp.bfloat16
STREAMS = 2
ROWS = 128


def place():
    b = lax.axis_index("batch")
    t = lax.axis_index("tensor")
    return b // 8, (b // 4) % 2, b % 4, t // 2, t % 2


def device(z, l, y, h, c):
    return (z * 8 + l * 4 + y, h * 2 + c)


def remote(src, dst, send_sem, recv_sem, dev):
    return pltpu.make_async_remote_copy(
        src_ref=src, dst_ref=dst, send_sem=send_sem, recv_sem=recv_sem, device_id=dev, device_id_type=MESH
    )


def greet(devices):
    barrier = pltpu.get_barrier_semaphore()
    for dev in devices:
        pl.semaphore_signal(barrier, inc=1, device_id=dev, device_id_type=MESH)
    return lambda: pl.semaphore_wait(barrier, len(devices))


def batch_peers(z, l, y, h, c):
    peers = [device(z, 1 - l, y, h, c)]
    peers += [device(z, l, (y + d) % 4, h, c) for d in (1, 2, 3)]
    peers += [device((z + d) % 4, l, y, h, c) for d in (1, 2, 3)]
    return peers


def net_kernel(
    x_ref, wn_hbm, steps_ref, bg_ref, be_hbm, bc_ref, br_hbm, bt_ref, bn_ref, fg_ref, fe_hbm, fc_ref, fr_hbm,
    walk_ref, ge_ref, gr_ref,
    be, br, fe, fr, wn, u, nb, ab, pcs, pcr, pfs, pfr, own, flow, hid, tau, m0, m1, m2, m3,
    err_ref, normh, act_ref, hg_ref, pn, ph,
    gy_r, gz_r, r1y_r, r1z_r, ay_r, az_r, r2_r, b_r, s_r, r3_r,
    gy_e, gz_e, r1y_e, r1z_e, ay_e, az_e, r2_e,
    load_sem, ss, rs, ms, mr, gs, gr,
):
    z, l, y, h, c = place()
    core_dev = device(z, l, y, h, 1 - c)
    far_dev = device(z, l, y, 1 - h, c)
    q_own, q_far = 2 * h + c, 2 * (1 - h) + c

    loads = [
        pltpu.make_async_copy(src, dst, load_sem.at[i])
        for i, (src, dst) in enumerate(((be_hbm, be), (br_hbm, br), (wn_hbm, wn), (fe_hbm, fe), (fr_hbm, fr)))
    ]
    for load in loads:
        load.start()
    arrived = greet([core_dev, far_dev] + batch_peers(z, l, y, h, c))

    def rows(s):
        return slice(s * ROWS, (s + 1) * ROWS)

    def ag_core(s):
        return remote(u.at[s, q_own], u.at[s, q_own], ss.at[0, s], rs.at[0, s], core_dev)

    def ag_far(s):
        return remote(u.at[s, q_own], u.at[s, q_own], ss.at[1, s], rs.at[1, s], far_dev)

    def ag_fwd(s):
        return remote(u.at[s, q_far], u.at[s, q_far], ss.at[2, s], rs.at[2, s], core_dev)

    def rs_core(s, i):
        side = (1 - h) if i == 0 else h
        return remote(pcs.at[s, side], pcr.at[s, side], ss.at[3 + i, s], rs.at[3 + i, s], core_dev)

    def rs_far(s):
        return remote(pfs.at[s], pfr.at[s], ss.at[5, s], rs.at[5, s], far_dev)

    def gather_start(s):
        ag_far(s).start()
        ag_core(s).start()

    def gather_wait(s):
        ag_far(s).wait_recv()
        ag_fwd(s).start()
        ag_core(s).wait_recv()
        ag_fwd(s).wait_recv()

    def put_own(s, value):
        ag_core(s).wait_send()
        ag_far(s).wait_send()
        u[s, q_own] = value.astype(BF16)

    def normalize(s, gain_ref):
        parts = [u[s, q].astype(F32) for q in range(4)]
        total = sum(jnp.sum(p * p, axis=1, keepdims=True) for p in parts)
        factor = lax.rsqrt(total * (1.0 / 2048.0) + EPSILON)
        for q in range(4):
            nb[:, 512 * q : 512 * (q + 1)] = (parts[q] * factor * gain_ref[:, 512 * q : 512 * (q + 1)]).astype(BF16)

    def reduce_start(s, active, reduce_ref):
        for i in range(2):
            side = (1 - h) if i == 0 else h
            column = pl.multiple_of((2 * side + 1 - c) * 512, 512)
            pcs[s, side] = jnp.dot(active, reduce_ref[:, pl.ds(column, 512)], preferred_element_type=F32)
            rs_core(s, i).start()
        part = jnp.dot(
            active, reduce_ref[:, pl.ds(pl.multiple_of(q_far * 512, 512), 512)], preferred_element_type=F32
        )
        rs_core(s, 0).wait_recv()
        ag_fwd(s).wait_send()
        pfs[s] = (part + pcr[s, 1 - h]).astype(BF16)
        rs_far(s).start()
        part = jnp.dot(
            active, reduce_ref[:, pl.ds(pl.multiple_of(q_own * 512, 512), 512)], preferred_element_type=F32
        )
        rs_core(s, 1).wait_recv()
        own[s] = part + pcr[s, h]
        rs_core(s, 0).wait_send()
        rs_core(s, 1).wait_send()

    def reduce_wait(s):
        rs_far(s).wait()
        return own[s] + pfr[s].astype(F32)

    for s in range(STREAMS):
        u[s, q_own] = x_ref[rows(s)]
        walk_ref[rows(s)] = x_ref[rows(s)].astype(F32)
    arrived()
    for s in range(STREAMS):
        gather_start(s)

    for s in range(STREAMS):
        noise = bn_ref[rows(s)].astype(F32).reshape(16, 8, 512)
        times = jnp.transpose(jnp.broadcast_to(bt_ref[s : s + 1, :], (128, 128)))
        high = times.astype(BF16).astype(F32)
        low = times - high
        packed = jnp.concatenate([noise[:, :, :256], noise[:, :, 256:]], axis=1)
        clocks = jnp.concatenate([high.reshape(16, 8, 128), low.reshape(16, 8, 128)], axis=1)
        m0[2 * s : 2 * s + 2] = (
            jnp.concatenate([packed, clocks], axis=2).astype(BF16).reshape(2, 2, 4, 16, 384)
        )

    def swap_l():
        return remote(m0.at[:, 1 - l], m1.at[:, l], ms.at[0], mr.at[0], device(z, 1 - l, y, h, c))

    def swap_y(d):
        to = (y + d) % 4
        return remote(m1.at[:, :, to], m2.at[:, :, y], ms.at[d], mr.at[d], device(z, l, to, h, c))

    def swap_z(d):
        to = (z + d) % 4
        return remote(m2.at[to], m3.at[z], ms.at[3 + d], mr.at[3 + d], device(to, l, y, h, c))

    swap_l().start()
    m1[:, l] = m0[:, l]

    loads[0].wait()
    loads[1].wait()
    loads[2].wait()

    def step(k, clock):
        width = steps_ref[k]
        for s in range(STREAMS):
            gather_wait(s)
            normalize(s, bg_ref)
            for n in range(4):
                cols = slice(256 * n, 256 * (n + 1))
                hidden = jnp.dot(nb[...], be[:, cols], preferred_element_type=F32) + clock * bc_ref[:, cols]
                ab[:, cols] = (hidden * jax.nn.sigmoid(hidden)).astype(BF16)
            reduce_start(s, ab[...], br)

        @pl.when(k == 0)
        def _():
            swap_l().wait()
            for d in (1, 2, 3):
                swap_y(d).start()
            m2[:, :, y] = m1[:, :, y]

        @pl.when(k == 1)
        def _():
            for d in (1, 2, 3):
                swap_y(d).wait()
            for d in (1, 2, 3):
                swap_z(d).start()
            m3[z] = m2[z]

        @pl.when(k == 3)
        def _():
            for d in (1, 2, 3):
                swap_z(d).wait()

        spread = jnp.sqrt(jnp.full((1, 512), width, F32)) * NOISE_LEVEL
        for s in range(STREAMS):
            drift = reduce_wait(s)
            state = walk_ref[rows(s)] - width * drift + spread * wn[k, rows(s)].astype(F32)
            walk_ref[rows(s)] = state

            @pl.when(k < 3)
            def _():
                put_own(s, state)

            @pl.when(k == 3)
            def _():
                message = m3[2 * s : 2 * s + 2].reshape(16, 16, 384).astype(F32)
                noise = jnp.concatenate(
                    [message[:, :8, :256].reshape(ROWS, 256), message[:, 8:, :256].reshape(ROWS, 256)], axis=1
                )
                times = (message[:, :8, 256:] + message[:, 8:, 256:]).reshape(ROWS, 128)
                tau[s] = times
                times = jnp.concatenate([times] * 4, axis=1)
                start = state.astype(BF16).astype(F32)
                end = x_ref[rows(s)].astype(F32)
                mixed = (1.0 - times) * start + times * end + jnp.sqrt(times * (1.0 - times)) * NOISE_LEVEL * noise
                flow[s] = (end - mixed) / (1.0 - times)
                put_own(s, mixed)

            gather_start(s)
        return clock - width

    lax.fori_loop(0, 4, step, jnp.float32(1.0))

    loads[3].wait()
    loads[4].wait()
    for s in range(STREAMS):
        gather_wait(s)
        normalize(s, fg_ref)
        for q in range(4):
            for i in range(2):
                normh[i, rows(s), 256 * q : 256 * (q + 1)] = nb[:, 512 * q + 256 * i : 512 * q + 256 * (i + 1)]
        times = jnp.concatenate([tau[s]] * 2, axis=1)
        for n in range(4):
            cols = slice(256 * n, 256 * (n + 1))
            hidden = jnp.dot(nb[...], fe[:, cols], preferred_element_type=F32) + times * fc_ref[:, cols]
            hid[s, :, cols] = hidden
            act_ref[rows(s), cols] = (hidden * jax.nn.sigmoid(hidden)).astype(BF16)
        reduce_start(s, act_ref[rows(s)], fr)
    scale = 1.0 / (8192.0**0.5)
    for s in range(STREAMS):
        put_own(s, (reduce_wait(s) - flow[s]) * scale)
        gather_start(s)
    for s in range(STREAMS):
        gather_wait(s)
        for q in range(4):
            err_ref[rows(s), 512 * q : 512 * (q + 1)] = u[s, q]

    pair_dev = device(z, 1 - l, y, h, c)
    share = pl.ds(pl.multiple_of(c * 128, 128), 128)

    def ydev(d):
        return device(z, l, (y + d) % 4, h, c)

    def zdev(d):
        return device((z + d) % 4, l, y, h, c)

    def pair_normed():
        return remote(normh.at[1 - l, share], pn.at[share], gs.at[26], gr.at[26], pair_dev)

    def pair_forward():
        return remote(pn.at[share], pn.at[share], gs.at[27], gr.at[27], core_dev)

    def pair_grad(s):
        return remote(hg_ref.at[rows(s)], ph.at[rows(s)], gs.at[28 + s], gr.at[28 + s], pair_dev)

    def r_first_y(d):
        return remote(gy_r.at[:, :, (y + d) % 4], r1y_r.at[d - 1], gs.at[d - 1], gr.at[d - 1], ydev(d))

    def r_first_z(d):
        return remote(gz_r.at[(z + d) % 4], r1z_r.at[d - 1], gs.at[2 + d], gr.at[2 + d], zdev(d))

    def r_second_y(d):
        return remote(ay_r.at[(z + d) % 4], r2_r.at[0, d - 1], gs.at[5 + d], gr.at[5 + d], zdev(d))

    def r_second_z(d):
        return remote(az_r.at[:, (y + d) % 4], r2_r.at[1, d - 1], gs.at[8 + d], gr.at[8 + d], ydev(d))

    def r_third(i):
        return remote(s_r.at[i], r3_r.at[i], gs.at[12 + i], gr.at[12 + i], pair_dev)

    def e_first_y(d):
        return remote(gy_e.at[:, (y + d) % 4], r1y_e.at[d - 1], gs.at[13 + d], gr.at[13 + d], ydev(d))

    def e_first_z(d):
        return remote(gz_e.at[(z + d) % 4], r1z_e.at[d - 1], gs.at[16 + d], gr.at[16 + d], zdev(d))

    def e_second_y(d):
        return remote(ay_e.at[(z + d) % 4], r2_e.at[0, d - 1], gs.at[19 + d], gr.at[19 + d], zdev(d))

    def e_second_z(d):
        return remote(az_e.at[(y + d) % 4], r2_e.at[1, d - 1], gs.at[22 + d], gr.at[22 + d], ydev(d))

    def outer(left, right):
        return lax.dot_general(left, right, (((0,), (0,)), ((), ())), preferred_element_type=F32)

    def make_r(to):
        def one(i, _):
            column = pl.multiple_of((to * 2 + i) * 256, 256)
            part = outer(err_ref[:, pl.ds(column, 256)], act_ref[...]).astype(BF16)
            gy_r[to, i] = part[:, :512].reshape(4, 64, 512)
            gz_r[to, i] = part[:, 512:].reshape(4, 64, 512)
            for d in (1, 2, 3):
                dst = (y + d) % 4
                remote(
                    gy_r.at[to, i, dst], r1y_r.at[d - 1, to, i], gs.at[d - 1], gr.at[d - 1], ydev(d)
                ).start()
            return 0

        lax.fori_loop(0, 2, one, 0)

    pair_normed().start()
    for d in (2, 1, 3, 0):
        make_r((z + d) % 4)
        if d:
            r_first_z(d).start()

    for s in range(STREAMS):
        for n in range(4):
            cols = slice(256 * n, 256 * (n + 1))
            back = lax.dot_general(
                err_ref[rows(s)], fr[cols, :], (((1,), (1,)), ((), ())), preferred_element_type=F32
            )
            hidden = hid[s, :, cols]
            sig = jax.nn.sigmoid(hidden)
            hg_ref[rows(s), cols] = (back * (sig * (1.0 + hidden * (1.0 - sig)))).astype(BF16)
        pair_grad(s).start()
    for s in range(STREAMS):
        ag_core(s).wait_send()
        ag_far(s).wait_send()
        ag_fwd(s).wait_send()

    pair_normed().wait()
    pair_forward().start()
    pair_forward().wait()
    for s in range(STREAMS):
        pair_grad(s).wait()

    def make_e(j, _):
        to = (z + 1 + j) % 4
        column = pl.ds(pl.multiple_of(to * 256, 256), 256)
        part = (outer(normh[l, :, column], hg_ref[...]) + outer(pn[:, column], ph[...])).astype(BF16)
        gy_e[to] = part[:, :512].reshape(4, 64, 512)
        gz_e[to] = part[:, 512:].reshape(4, 64, 512)
        for d in (1, 2, 3):
            dst = (y + d) % 4
            remote(
                gy_e.at[to, dst], r1y_e.at[d - 1, to], gs.at[13 + d], gr.at[13 + d], ydev(d)
            ).start()
        return 0

    for d in (1, 2, 3):
        lax.fori_loop(d - 1, d, make_e, 0)
        e_first_z(d).start()
    lax.fori_loop(3, 4, make_e, 0)

    for d in (1, 2, 3):
        r_first_y(d).wait()

    def add_ry(i, _):
        total = gy_r[i, :, y].astype(F32) + sum(r1y_r[d, i].astype(F32) for d in range(3))
        ay_r[i] = total.astype(BF16)
        return 0

    lax.fori_loop(0, 4, add_ry, 0)
    for d in (1, 2, 3):
        r_second_y(d).start()
    for d in (1, 2, 3):
        r_first_z(d).wait()

    def add_rz(i, _):
        total = gz_r[z, :, i].astype(F32) + sum(r1z_r[d, :, i].astype(F32) for d in range(3))
        az_r[:, i] = total.astype(BF16)
        return 0

    lax.fori_loop(0, 4, add_rz, 0)
    for d in (1, 2, 3):
        r_second_z(d).start()

    def finish_r(i):
        for d in (1, 2, 3):
            (r_second_y(d) if i == 0 else r_second_z(d)).wait()

        def own(side):
            return ay_r[z, side] if i == 0 else az_r[side, y]

        s_r[i] = (
            own(1 - l).astype(F32) + sum(r2_r[i, d, 1 - l].astype(F32) for d in range(3))
        ).astype(BF16)
        r_third(i).start()
        b_r[i] = own(l).astype(F32) + sum(r2_r[i, d, l].astype(F32) for d in range(3))

    finish_r(0)
    finish_r(1)

    for d in (1, 2, 3):
        e_first_y(d).wait()

    def add_ey(i, _):
        total = gy_e[i, y].astype(F32) + sum(r1y_e[d, i].astype(F32) for d in range(3))
        ay_e[i] = total.astype(BF16)
        return 0

    lax.fori_loop(0, 4, add_ey, 0)
    for d in (1, 2, 3):
        e_second_y(d).start()
    for d in (1, 2, 3):
        e_first_z(d).wait()

    def add_ez(i, _):
        total = gz_e[z, i].astype(F32) + sum(r1z_e[d, i].astype(F32) for d in range(3))
        az_e[i] = total.astype(BF16)
        return 0

    lax.fori_loop(0, 4, add_ez, 0)
    for d in (1, 2, 3):
        e_second_z(d).start()
    for i in range(2):
        r_third(i).wait()
        gr_ref[:, 512 * i : 512 * (i + 1)] = b_r[i] + r3_r[i].astype(F32)
    for i in range(2):
        for d in (1, 2, 3):
            (e_second_y(d) if i == 0 else e_second_z(d)).wait()
        mine = ay_e[z] if i == 0 else az_e[y]
        ge_ref[:, 512 * i : 512 * (i + 1)] = mine.astype(F32) + sum(r2_e[i, d].astype(F32) for d in range(3))


def copy_kernel(a_in, b_in, c_in, a_out, b_out, c_out, a_mid, b_mid, c_mid, sems):
    trios = ((a_in, a_mid, a_out), (b_in, b_mid, b_out), (c_in, c_mid, c_out))
    into = [pltpu.make_async_copy(src, mid, sems.at[0, i]) for i, (src, mid, dst) in enumerate(trios)]
    out = [pltpu.make_async_copy(mid, dst, sems.at[1, i]) for i, (src, mid, dst) in enumerate(trios)]
    for copy in into:
        copy.start()
    for first, second in zip(into, out):
        first.wait()
        second.start()
    for copy in out:
        copy.wait()


def body(
    target_latents, walk_noise, step_sizes, back_gain, back_expand, back_clock, back_reduce,
    bridge_times, bridge_noise, fore_gain, fore_expand, fore_clock, fore_reduce,
):
    vmem = pl.BlockSpec(memory_space=pltpu.VMEM)
    smem = pl.BlockSpec(memory_space=pltpu.SMEM)
    hbm = pl.BlockSpec(memory_space=pl.ANY)
    dma = pltpu.SemaphoreType.DMA
    sds = jax.ShapeDtypeStruct
    S, R = STREAMS, ROWS
    outs = pl.pallas_call(
        net_kernel,
        out_shape=(sds((256, 512), F32), sds((64, 1024), F32), sds((64, 1024), F32)),
        in_specs=[vmem, hbm, smem, vmem, hbm, vmem, hbm, vmem, vmem, vmem, hbm, vmem, hbm],
        out_specs=(vmem,) * 3,
        scratch_shapes=[
            pltpu.VMEM((2048, 1024), BF16), pltpu.VMEM((1024, 2048), BF16),
            pltpu.VMEM((2048, 1024), BF16), pltpu.VMEM((1024, 2048), BF16),
            pltpu.VMEM((4, 256, 512), BF16),
            pltpu.VMEM((S, 4, R, 512), BF16),
            pltpu.VMEM((R, 2048), BF16), pltpu.VMEM((R, 1024), BF16),
            pltpu.VMEM((S, 2, R, 512), F32), pltpu.VMEM((S, 2, R, 512), F32),
            pltpu.VMEM((S, R, 512), BF16), pltpu.VMEM((S, R, 512), BF16),
            pltpu.VMEM((S, R, 512), F32), pltpu.VMEM((S, R, 512), F32),
            pltpu.VMEM((S, R, 1024), F32), pltpu.VMEM((S, R, 128), F32),
        ]
        + [pltpu.VMEM((4, 2, 4, 16, 384), BF16)] * 4
        + [
            pltpu.VMEM((256, 2048), BF16), pltpu.VMEM((2, 256, 1024), BF16),
            pltpu.VMEM((256, 1024), BF16), pltpu.VMEM((256, 1024), BF16),
            pltpu.VMEM((256, 1024), BF16), pltpu.VMEM((256, 1024), BF16),
            pltpu.VMEM((4, 2, 4, 64, 512), BF16), pltpu.VMEM((4, 2, 4, 64, 512), BF16),
            pltpu.VMEM((3, 4, 2, 64, 512), BF16), pltpu.VMEM((3, 2, 4, 64, 512), BF16),
            pltpu.VMEM((4, 2, 64, 512), BF16), pltpu.VMEM((2, 4, 64, 512), BF16),
            pltpu.VMEM((2, 3, 2, 64, 512), BF16),
            pltpu.VMEM((2, 64, 512), F32), pltpu.VMEM((2, 64, 512), BF16), pltpu.VMEM((2, 64, 512), BF16),
            pltpu.VMEM((4, 4, 64, 512), BF16), pltpu.VMEM((4, 4, 64, 512), BF16),
            pltpu.VMEM((3, 4, 64, 512), BF16), pltpu.VMEM((3, 4, 64, 512), BF16),
            pltpu.VMEM((4, 64, 512), BF16), pltpu.VMEM((4, 64, 512), BF16),
            pltpu.VMEM((2, 3, 64, 512), BF16),
        ]
        + [dma((5,)), dma((6, S)), dma((6, S)), dma((7,)), dma((7,)), dma((30,)), dma((30,))],
        compiler_params=pltpu.CompilerParams(
            collective_id=0, has_side_effects=True, vmem_limit_bytes=58 * 2**20
        ),
        name="net",
    )(
        target_latents, walk_noise, step_sizes, back_gain.reshape(1, 2048), back_expand,
        back_clock.reshape(1, 1024), back_reduce, bridge_times.reshape(2, 128), bridge_noise,
        fore_gain.reshape(1, 2048), fore_expand, fore_clock.reshape(1, 1024), fore_reduce,
    )
    return pl.pallas_call(
        copy_kernel,
        out_shape=tuple(sds(o.shape, o.dtype) for o in outs),
        in_specs=[hbm] * 3,
        out_specs=(hbm,) * 3,
        scratch_shapes=[pltpu.VMEM(o.shape, o.dtype) for o in outs] + [dma((2, 3))],
        name="place_outputs",
    )(*outs)


def solution(mesh):
    placed = (
        P("batch", "tensor"), P(None, "batch", "tensor"), P(), P(), P(None, "tensor"), P("tensor"),
        P("tensor", None), P("batch"), P("batch", "tensor"), P(), P(None, "tensor"), P("tensor"),
        P("tensor", None),
    )
    return jax.shard_map(
        body, mesh=mesh, in_specs=placed,
        out_specs=(P("batch", "tensor"), P("batch", "tensor"), P("batch", "tensor")), check_vma=False,
    )
```

```python
import jax
import jax.numpy as jnp
from jax import lax
from jax.experimental import pallas as pl
from jax.experimental.pallas import tpu as pltpu
from jax.sharding import PartitionSpec as P

NOISE_LEVEL = 0.5
EPSILON = 1e-06
MESH = pl.DeviceIdType.MESH
F32 = jnp.float32
BF16 = jnp.bfloat16
ROWS = 128


def place():
    b = lax.axis_index("batch")
    t = lax.axis_index("tensor")
    return b // 8, (b // 4) % 2, b % 4, t // 2, t % 2


def device(z, l, y, h, c):
    return (z * 8 + l * 4 + y, h * 2 + c)


def remote(src, dst, send_sem, recv_sem, dev):
    return pltpu.make_async_remote_copy(
        src_ref=src, dst_ref=dst, send_sem=send_sem, recv_sem=recv_sem, device_id=dev, device_id_type=MESH
    )


def greet(devices):
    barrier = pltpu.get_barrier_semaphore()
    for dev in devices:
        pl.semaphore_signal(barrier, inc=1, device_id=dev, device_id_type=MESH)
    return lambda: pl.semaphore_wait(barrier, len(devices))


def batch_peers(z, l, y, h, c):
    peers = [device(z, 1 - l, y, h, c)]
    peers += [device(z, l, (y + d) % 4, h, c) for d in (1, 2, 3)]
    peers += [device((z + d) % 4, l, y, h, c) for d in (1, 2, 3)]
    return peers


def net_kernel(
    x_ref, wn_hbm, steps_ref, bg_ref, be_hbm, bc_ref, br_hbm, bt_ref, bn_ref, fg_ref, fe_hbm, fc_ref, fr_hbm,
    walk_ref, ge_ref, gr_ref,
    be, br, fe, fr, bca, fca, wn, xt, u, st, acc, ab, own, pfs, pfr, flow, m0, m1, m2, m3, mf, wx,
    err, normh, act_ref, hg_ref, hs, pn, ph,
    gy_r, gz_r, r1y_r, r1z_r, ay_r, az_r, r2_r, b_r, s_r, r3_r,
    gy_e, gz_e, r1y_e, r1z_e, ay_e, az_e, r2_e,
    load_sem, cs, cr, fs, fr_sem, ms, mr, gs, gr,
):
    z, l, y, h, c = place()
    core_dev = device(z, l, y, h, 1 - c)
    far_dev = device(z, l, y, 1 - h, c)
    pair_dev = device(z, 1 - l, y, h, c)
    share = pl.ds(pl.multiple_of(c * 128, 128), 128)
    other = pl.ds(pl.multiple_of((1 - c) * 128, 128), 128)

    def load(i):
        src, dst = (
            (be_hbm, be.at[c]), (br_hbm, br.at[c]), (fe_hbm, fe.at[c]), (fr_hbm, fr.at[c]),
            (wn_hbm.at[:, share], wn.at[c]),
        )[i]
        return pltpu.make_async_copy(src, dst, load_sem.at[i])

    def cross(i):
        src, dst = (
            (be_hbm, be.at[c]), (br_hbm, br.at[c]), (fe_hbm, fe.at[c]), (fr_hbm, fr.at[c]),
            (wn_hbm.at[:, other], wn.at[c]),
            (x_ref.at[other], xt.at[c]),
            (bca.at[c], bca.at[c]), (fca.at[c], fca.at[c]),
            (m3.at[pl.ds(2 * (1 - c), 2)], mf.at[c]),
            (st.at[pl.ds(2 * (1 - c), 2)], wx),
            (ab.at[1 - c], act_ref.at[share]),
            (normh.at[:, share], normh.at[:, share]),
            (hs, hg_ref.at[share]),
        )[i]
        return remote(src, dst, cs.at[i], cr.at[i], core_dev)

    def cross_err(j, i):
        return remote(err.at[j, share], err.at[j, share], cs.at[13 + i], cr.at[13 + i], core_dev)

    def gather(i):
        return remote(u.at[4 * h + i], u.at[4 * h + i], fs.at[i], fr_sem.at[i], far_dev)

    def reduce(i):
        return remote(pfs.at[i], pfr.at[i], fs.at[4 + i], fr_sem.at[4 + i], far_dev)

    def gather_err(i):
        j = 4 * h + i
        return remote(err.at[j, share], err.at[j, share], fs.at[8 + i], fr_sem.at[8 + i], far_dev)

    for i in (0, 1, 4):
        load(i).start()
    arrived = greet([core_dev, far_dev] + batch_peers(z, l, y, h, c))
    bca[c] = bc_ref[...]
    fca[c] = fc_ref[...]
    for i in range(2):
        u[4 * h + 2 * c + i] = x_ref[share, 256 * i : 256 * (i + 1)]
    xt[c] = x_ref[share]
    arrived()
    cross(5).start()
    for i in range(2):
        gather(2 * c + i).start()
    cross(6).start()
    cross(0).start()
    cross(7).start()
    cross(5).wait()
    for i in range(2):
        u[4 * h + 2 * (1 - c) + i] = xt[1 - c, :, 256 * i : 256 * (i + 1)]
        gather(2 * (1 - c) + i).start()
    cross(1).start()
    cross(4).start()
    for i in range(4):
        st[i] = u[4 * h + i].astype(F32)

    for s in range(2):
        noise = bn_ref[128 * s : 128 * (s + 1)].astype(F32).reshape(16, 8, 512)
        times = jnp.transpose(jnp.broadcast_to(bt_ref[s : s + 1, :], (128, 128)))
        high = times.astype(BF16).astype(F32)
        low = times - high
        packed = jnp.concatenate([noise[:, :, :256], noise[:, :, 256:]], axis=1)
        clocks = jnp.concatenate([high.reshape(16, 8, 128), low.reshape(16, 8, 128)], axis=1)
        m0[2 * s : 2 * s + 2] = (
            jnp.concatenate([packed, clocks], axis=2).astype(BF16).reshape(2, 2, 4, 16, 384)
        )

    def swap_l():
        return remote(m0.at[:, 1 - l], m1.at[:, l], ms.at[0], mr.at[0], pair_dev)

    def swap_y(d):
        to = (y + d) % 4
        return remote(m1.at[:, :, to], m2.at[:, :, y], ms.at[d], mr.at[d], device(z, l, to, h, c))

    def swap_z(d):
        to = (z + d) % 4
        return remote(m2.at[to], m3.at[z], ms.at[3 + d], mr.at[3 + d], device(to, l, y, h, c))

    swap_l().start()
    m1[:, l] = m0[:, l]

    def scaled(j, gain_ref):
        rows = u[j].astype(F32)
        return jnp.sum(rows * rows, axis=1, keepdims=True), (rows * gain_ref[j]).astype(BF16)

    def expand(gain_ref, weights, finish):
        squares = jnp.zeros((ROWS, 1), F32)
        near = []
        for i in range(4):
            square, part = scaled(4 * h + i, gain_ref)
            squares += square
            near.append(part)
        near = jnp.concatenate(near, axis=1)
        near_rows = pl.ds(pl.multiple_of(h * 1024, 1024), 1024)
        for q in range(2):
            for n in range(4):
                cols = slice(256 * n, 256 * (n + 1))
                acc[q, :, cols] = jnp.dot(near, weights[q, near_rows, cols], preferred_element_type=F32)
        for i in range(4):
            gather(i).wait_recv()
            j = 4 * (1 - h) + i
            square, part = scaled(j, gain_ref)
            squares += square
            far_rows = pl.ds(pl.multiple_of(j * 256, 256), 256)
            if i == 3:
                factor = lax.rsqrt(squares * (1.0 / 2048.0) + EPSILON)
            for q in range(2):
                for n in range(4):
                    cols = slice(256 * n, 256 * (n + 1))
                    total = acc[q, :, cols] + jnp.dot(part, weights[q, far_rows, cols], preferred_element_type=F32)
                    if i < 3:
                        acc[q, :, cols] = total
                    else:
                        finish(q, cols, total * factor)
        return factor

    def contract(weights, j):
        cols = pl.ds(pl.multiple_of(j * 256, 256), 256)
        return jnp.dot(ab[0], weights[0, :, cols], preferred_element_type=F32) + jnp.dot(
            ab[1], weights[1, :, cols], preferred_element_type=F32
        )

    def reduce_start(weights):
        for i in range(4):
            pfs[i] = contract(weights, 4 * (1 - h) + i).astype(BF16)
            reduce(i).start()
        for i in range(4):
            own[i] = contract(weights, 4 * h + i)

    def reduce_wait(i):
        reduce(i).wait()
        return own[i] + pfr[i].astype(F32)

    for i in (0, 1, 4):
        load(i).wait()
    cross(0).wait()
    cross(6).wait()
    cross(7).wait()

    def step(k, clock):
        width = steps_ref[k]

        def finish(q, cols, product):
            hidden = product + clock * bca[q, :, cols]
            ab[q, :, cols] = (hidden * jax.nn.sigmoid(hidden)).astype(BF16)

        expand(bg_ref, be, finish)

        @pl.when(k == 0)
        def _():
            cross(1).wait()

        reduce_start(br)

        @pl.when(k == 0)
        def _():
            cross(4).wait()
            for i in (2, 3):
                load(i).start()
            cross(2).start()
            swap_l().wait()
            for d in (1, 2, 3):
                swap_y(d).start()
            m2[:, :, y] = m1[:, :, y]

        @pl.when(k == 1)
        def _():
            cross(3).start()
            for d in (1, 2, 3):
                swap_y(d).wait()
            for d in (1, 2, 3):
                swap_z(d).start()
            m3[z] = m2[z]

        @pl.when(k == 2)
        def _():
            for d in (1, 2, 3):
                swap_z(d).wait()
            cross(8).start()
            mf[c] = m3[pl.ds(2 * c, 2)]

        @pl.when(k == 3)
        def _():
            cross(8).wait()

        spread = jnp.sqrt(jnp.full((1, 256), width, F32)) * NOISE_LEVEL
        for i in range(4):
            q, cols = i // 2, slice(256 * (i % 2), 256 * (i % 2) + 256)
            state = st[i] - width * reduce_wait(i) + spread * wn[q, k, :, cols].astype(F32)
            st[i] = state
            gather(i).wait_send()

            @pl.when(k != 3)
            def _():
                u[4 * h + i] = state.astype(BF16)

            @pl.when(k == 3)
            def _():
                message = mf[q].reshape(16, 16, 384).astype(F32)
                half = slice(8 * (i % 2), 8 * (i % 2) + 8)
                noise = message[:, half, :256].reshape(ROWS, 256)
                times = (message[:, :8, 256:] + message[:, 8:, 256:]).reshape(ROWS, 128)
                times = jnp.concatenate([times] * 2, axis=1)
                start = state.astype(BF16).astype(F32)
                end = xt[q, :, cols].astype(F32)
                mixed = (1.0 - times) * start + times * end + jnp.sqrt(times * (1.0 - times)) * NOISE_LEVEL * noise
                flow[i] = (end - mixed) / (1.0 - times)
                u[4 * h + i] = mixed.astype(BF16)

            gather(i).start()
        return clock - width

    lax.fori_loop(0, 4, step, jnp.float32(1.0))

    for i in (2, 3):
        load(i).wait()
        cross(i).wait()
    cross(9).start()
    message = mf[0].reshape(16, 16, 384)[:, :, 256:].astype(F32)
    times = (message[:, :8] + message[:, 8:]).reshape(ROWS, 128)
    times = jnp.concatenate([times] * 2, axis=1)

    def finish_fore(q, cols, product):
        hidden = product + times * fca[q, :, cols]
        acc[q, :, cols] = hidden
        ab[q, :, cols] = (hidden * jax.nn.sigmoid(hidden)).astype(BF16)

    factor = expand(fg_ref, fe, finish_fore)
    reduce_start(fr)
    act_ref[share] = ab[c]
    cross(10).start()
    for j in range(8):
        normh[j % 2, share, 256 * (j // 2) : 256 * (j // 2 + 1)] = (
            u[j].astype(F32) * factor * fg_ref[j]
        ).astype(BF16)
    cross(11).start()
    cross(9).wait()
    for i in range(2):
        walk_ref[share, 256 * i : 256 * (i + 1)] = st[2 * c + i]
        walk_ref[other, 256 * i : 256 * (i + 1)] = wx[i]
    scale = 1.0 / (8192.0**0.5)
    for i in range(4):
        j = 4 * h + i
        err[j, share] = ((reduce_wait(i) - flow[i]) * scale).astype(BF16)
        gather_err(i).start()
        cross_err(j, i).start()
    for i in range(4):
        gather(i).wait_send()
    cross(10).wait()
    cross(11).wait()

    def pair_normed():
        return remote(normh.at[1 - l, share], pn.at[share], gs.at[26], gr.at[26], pair_dev)

    def ydev(d):
        return device(z, l, (y + d) % 4, h, c)

    def zdev(d):
        return device((z + d) % 4, l, y, h, c)

    def pair_forward():
        return remote(pn.at[share], pn.at[share], gs.at[27], gr.at[27], core_dev)

    def pair_grad(s):
        part = share if s == 0 else other
        return remote(hg_ref.at[part], ph.at[part], gs.at[28 + s], gr.at[28 + s], pair_dev)

    def r_first_y(d):
        return remote(gy_r.at[:, :, (y + d) % 4], r1y_r.at[d - 1], gs.at[d - 1], gr.at[d - 1], ydev(d))

    def r_first_z(d):
        return remote(gz_r.at[(z + d) % 4], r1z_r.at[d - 1], gs.at[2 + d], gr.at[2 + d], zdev(d))

    def r_second_y(d):
        return remote(ay_r.at[(z + d) % 4], r2_r.at[0, d - 1], gs.at[5 + d], gr.at[5 + d], zdev(d))

    def r_second_z(d):
        return remote(az_r.at[:, (y + d) % 4], r2_r.at[1, d - 1], gs.at[8 + d], gr.at[8 + d], ydev(d))

    def r_third(i):
        return remote(s_r.at[i], r3_r.at[i], gs.at[12 + i], gr.at[12 + i], pair_dev)

    def e_first_y(d):
        return remote(gy_e.at[:, (y + d) % 4], r1y_e.at[d - 1], gs.at[13 + d], gr.at[13 + d], ydev(d))

    def e_first_z(d):
        return remote(gz_e.at[(z + d) % 4], r1z_e.at[d - 1], gs.at[16 + d], gr.at[16 + d], zdev(d))

    def e_second_y(d):
        return remote(ay_e.at[(z + d) % 4], r2_e.at[0, d - 1], gs.at[19 + d], gr.at[19 + d], zdev(d))

    def e_second_z(d):
        return remote(az_e.at[(y + d) % 4], r2_e.at[1, d - 1], gs.at[22 + d], gr.at[22 + d], ydev(d))

    def outer(left, right):
        return lax.dot_general(left, right, (((0,), (0,)), ((), ())), preferred_element_type=F32)

    def make_r(to):
        for i in range(2):
            part = outer(err[2 * to + i], act_ref[...]).astype(BF16)
            gy_r[to, i] = part[:, :512].reshape(4, 64, 512)
            gz_r[to, i] = part[:, 512:].reshape(4, 64, 512)
            for d in (1, 2, 3):
                dst = (y + d) % 4
                remote(
                    gy_r.at[to, i, dst], r1y_r.at[d - 1, to, i], gs.at[d - 1], gr.at[d - 1], ydev(d)
                ).start()
        for d in (1, 2, 3):

            @pl.when(to == (z + d) % 4)
            def _():
                r_first_z(d).start()

    for half in range(2):
        for i in range(2):
            cross_err(4 * h + 2 * half + i, 2 * half + i).wait_recv()
        make_r(2 * h + half)
    for i in range(4):
        gather_err(i).wait_recv()
        cross_err(4 * (1 - h) + i, 4 + i).start()
    pair_normed().start()
    for half in range(2):
        for i in range(2):
            cross_err(4 * (1 - h) + 2 * half + i, 4 + 2 * half + i).wait_recv()
        make_r(2 * (1 - h) + half)

    rows_err = jnp.concatenate([err[j, share] for j in range(8)], axis=1)
    for k in range(2):
        q = c if k == 0 else 1 - c
        for n in range(4):
            cols = slice(256 * n, 256 * (n + 1))
            back = lax.dot_general(
                rows_err, fr[q, cols, :], (((1,), (1,)), ((), ())), preferred_element_type=F32
            )
            hidden = acc[q, :, cols]
            sig = jax.nn.sigmoid(hidden)
            value = (back * (sig * (1.0 + hidden * (1.0 - sig)))).astype(BF16)
            if k == 0:
                hg_ref[share, cols] = value
            else:
                hs[:, cols] = value
        if k == 0:
            pair_grad(0).start()
        else:
            cross(12).start()
    cross(12).wait()
    pair_grad(1).start()
    for i in range(4):
        gather_err(i).wait_send()
        cross_err(4 * h + i, i).wait_send()
        cross_err(4 * (1 - h) + i, 4 + i).wait_send()

    pair_normed().wait()
    pair_forward().start()
    pair_forward().wait()
    for s in range(2):
        pair_grad(s).wait()

    def make_e(j, _):
        to = (z + 1 + j) % 4
        column = pl.ds(pl.multiple_of(to * 256, 256), 256)
        part = (outer(normh[l, :, column], hg_ref[...]) + outer(pn[:, column], ph[...])).astype(BF16)
        gy_e[to] = part[:, :512].reshape(4, 64, 512)
        gz_e[to] = part[:, 512:].reshape(4, 64, 512)
        for d in (1, 2, 3):
            dst = (y + d) % 4
            remote(
                gy_e.at[to, dst], r1y_e.at[d - 1, to], gs.at[13 + d], gr.at[13 + d], ydev(d)
            ).start()
        return 0

    for d in (1, 2, 3):
        lax.fori_loop(d - 1, d, make_e, 0)
        e_first_z(d).start()
    lax.fori_loop(3, 4, make_e, 0)

    for d in (1, 2, 3):
        r_first_y(d).wait()

    def add_ry(i, _):
        total = gy_r[i, :, y].astype(F32) + sum(r1y_r[d, i].astype(F32) for d in range(3))
        ay_r[i] = total.astype(BF16)
        return 0

    lax.fori_loop(0, 4, add_ry, 0)
    for d in (1, 2, 3):
        r_second_y(d).start()
    for d in (1, 2, 3):
        r_first_z(d).wait()

    def add_rz(i, _):
        total = gz_r[z, :, i].astype(F32) + sum(r1z_r[d, :, i].astype(F32) for d in range(3))
        az_r[:, i] = total.astype(BF16)
        return 0

    lax.fori_loop(0, 4, add_rz, 0)
    for d in (1, 2, 3):
        r_second_z(d).start()

    def finish_r(i):
        for d in (1, 2, 3):
            (r_second_y(d) if i == 0 else r_second_z(d)).wait()

        def own(side):
            return ay_r[z, side] if i == 0 else az_r[side, y]

        s_r[i] = (
            own(1 - l).astype(F32) + sum(r2_r[i, d, 1 - l].astype(F32) for d in range(3))
        ).astype(BF16)
        r_third(i).start()
        b_r[i] = own(l).astype(F32) + sum(r2_r[i, d, l].astype(F32) for d in range(3))

    finish_r(0)
    finish_r(1)

    for d in (1, 2, 3):
        e_first_y(d).wait()

    def add_ey(i, _):
        total = gy_e[i, y].astype(F32) + sum(r1y_e[d, i].astype(F32) for d in range(3))
        ay_e[i] = total.astype(BF16)
        return 0

    lax.fori_loop(0, 4, add_ey, 0)
    for d in (1, 2, 3):
        e_second_y(d).start()
    for d in (1, 2, 3):
        e_first_z(d).wait()

    def add_ez(i, _):
        total = gz_e[z, i].astype(F32) + sum(r1z_e[d, i].astype(F32) for d in range(3))
        az_e[i] = total.astype(BF16)
        return 0

    lax.fori_loop(0, 4, add_ez, 0)
    for d in (1, 2, 3):
        e_second_z(d).start()
    for i in range(2):
        r_third(i).wait()
        gr_ref[:, 512 * i : 512 * (i + 1)] = b_r[i] + r3_r[i].astype(F32)
    for i in range(2):
        for d in (1, 2, 3):
            (e_second_y(d) if i == 0 else e_second_z(d)).wait()
        mine = ay_e[z] if i == 0 else az_e[y]
        ge_ref[:, 512 * i : 512 * (i + 1)] = mine.astype(F32) + sum(r2_e[i, d].astype(F32) for d in range(3))


def copy_kernel(a_in, b_in, c_in, a_out, b_out, c_out, a_mid, b_mid, c_mid, sems):
    trios = ((a_in, a_mid, a_out), (b_in, b_mid, b_out), (c_in, c_mid, c_out))
    into = [pltpu.make_async_copy(src, mid, sems.at[0, i]) for i, (src, mid, dst) in enumerate(trios)]
    out = [pltpu.make_async_copy(mid, dst, sems.at[1, i]) for i, (src, mid, dst) in enumerate(trios)]
    for copy in into:
        copy.start()
    for first, second in zip(into, out):
        first.wait()
        second.start()
    for copy in out:
        copy.wait()


def body(
    target_latents, walk_noise, step_sizes, back_gain, back_expand, back_clock, back_reduce,
    bridge_times, bridge_noise, fore_gain, fore_expand, fore_clock, fore_reduce,
):
    vmem = pl.BlockSpec(memory_space=pltpu.VMEM)
    smem = pl.BlockSpec(memory_space=pltpu.SMEM)
    hbm = pl.BlockSpec(memory_space=pl.ANY)
    dma = pltpu.SemaphoreType.DMA
    sds = jax.ShapeDtypeStruct
    R = ROWS
    outs = pl.pallas_call(
        net_kernel,
        out_shape=(sds((256, 512), F32), sds((64, 1024), F32), sds((64, 1024), F32)),
        in_specs=[vmem, hbm, smem, vmem, hbm, vmem, hbm, vmem, vmem, vmem, hbm, vmem, hbm],
        out_specs=(vmem,) * 3,
        scratch_shapes=[
            pltpu.VMEM((2, 2048, 1024), BF16), pltpu.VMEM((2, 1024, 2048), BF16),
            pltpu.VMEM((2, 2048, 1024), BF16), pltpu.VMEM((2, 1024, 2048), BF16),
            pltpu.VMEM((2, 1, 1024), F32), pltpu.VMEM((2, 1, 1024), F32),
            pltpu.VMEM((2, 4, R, 512), BF16), pltpu.VMEM((2, R, 512), BF16),
            pltpu.VMEM((8, R, 256), BF16), pltpu.VMEM((4, R, 256), F32),
            pltpu.VMEM((2, R, 1024), F32), pltpu.VMEM((2, R, 1024), BF16),
            pltpu.VMEM((4, R, 256), F32), pltpu.VMEM((4, R, 256), BF16), pltpu.VMEM((4, R, 256), BF16),
            pltpu.VMEM((4, R, 256), F32),
        ]
        + [pltpu.VMEM((4, 2, 4, 16, 384), BF16)] * 4
        + [
            pltpu.VMEM((2, 2, 2, 4, 16, 384), BF16), pltpu.VMEM((2, R, 256), F32),
            pltpu.VMEM((8, 256, 256), BF16), pltpu.VMEM((2, 256, 1024), BF16),
            pltpu.VMEM((256, 1024), BF16), pltpu.VMEM((256, 1024), BF16), pltpu.VMEM((R, 1024), BF16),
            pltpu.VMEM((256, 1024), BF16), pltpu.VMEM((256, 1024), BF16),
            pltpu.VMEM((4, 2, 4, 64, 512), BF16), pltpu.VMEM((4, 2, 4, 64, 512), BF16),
            pltpu.VMEM((3, 4, 2, 64, 512), BF16), pltpu.VMEM((3, 2, 4, 64, 512), BF16),
            pltpu.VMEM((4, 2, 64, 512), BF16), pltpu.VMEM((2, 4, 64, 512), BF16),
            pltpu.VMEM((2, 3, 2, 64, 512), BF16),
            pltpu.VMEM((2, 64, 512), F32), pltpu.VMEM((2, 64, 512), BF16), pltpu.VMEM((2, 64, 512), BF16),
            pltpu.VMEM((4, 4, 64, 512), BF16), pltpu.VMEM((4, 4, 64, 512), BF16),
            pltpu.VMEM((3, 4, 64, 512), BF16), pltpu.VMEM((3, 4, 64, 512), BF16),
            pltpu.VMEM((4, 64, 512), BF16), pltpu.VMEM((4, 64, 512), BF16),
            pltpu.VMEM((2, 3, 64, 512), BF16),
        ]
        + [dma((5,)), dma((21,)), dma((21,)), dma((12,)), dma((12,)), dma((7,)), dma((7,)), dma((30,)), dma((30,))],
        compiler_params=pltpu.CompilerParams(
            collective_id=0, has_side_effects=True, vmem_limit_bytes=62 * 2**20
        ),
        name="net",
    )(
        target_latents, walk_noise, step_sizes, back_gain.reshape(8, 1, 256), back_expand,
        back_clock.reshape(1, 1024), back_reduce, bridge_times.reshape(2, 128), bridge_noise,
        fore_gain.reshape(8, 1, 256), fore_expand, fore_clock.reshape(1, 1024), fore_reduce,
    )
    return pl.pallas_call(
        copy_kernel,
        out_shape=tuple(sds(o.shape, o.dtype) for o in outs),
        in_specs=[hbm] * 3,
        out_specs=(hbm,) * 3,
        scratch_shapes=[pltpu.VMEM(o.shape, o.dtype) for o in outs] + [dma((2, 3))],
        name="place_outputs",
    )(*outs)


def solution(mesh):
    placed = (
        P("batch", "tensor"), P(None, "batch", "tensor"), P(), P(), P(None, "tensor"), P("tensor"),
        P("tensor", None), P("batch"), P("batch", "tensor"), P(), P(None, "tensor"), P("tensor"),
        P("tensor", None),
    )
    return jax.shard_map(
        body, mesh=mesh, in_specs=placed,
        out_specs=(P("batch", "tensor"), P("batch", "tensor"), P("batch", "tensor")), check_vma=False,
    )
```

```python
import jax
import jax.numpy as jnp
from jax import lax
from jax.experimental import pallas as pl
from jax.experimental.pallas import tpu as pltpu
from jax.sharding import PartitionSpec as P

NOISE_LEVEL = 0.5
EPSILON = 1e-06
MESH = pl.DeviceIdType.MESH
F32 = jnp.float32
BF16 = jnp.bfloat16
ROWS = 128
WIDE = 640
NARROW = 384


def place():
    b = lax.axis_index("batch")
    t = lax.axis_index("tensor")
    return b // 8, (b // 4) % 2, b % 4, t // 2, t % 2


def device(z, l, y, h, c):
    return (z * 8 + l * 4 + y, h * 2 + c)


def remote(src, dst, send_sem, recv_sem, dev):
    return pltpu.make_async_remote_copy(
        src_ref=src, dst_ref=dst, send_sem=send_sem, recv_sem=recv_sem, device_id=dev, device_id_type=MESH
    )


def greet(devices):
    barrier = pltpu.get_barrier_semaphore()
    for dev in devices:
        pl.semaphore_signal(barrier, inc=1, device_id=dev, device_id_type=MESH)
    return lambda: pl.semaphore_wait(barrier, len(devices))


def batch_peers(z, l, y, h, c):
    peers = [device(z, 1 - l, y, h, c)]
    peers += [device(z, l, (y + d) % 4, h, c) for d in (1, 2, 3)]
    peers += [device((z + d) % 4, l, y, h, c) for d in (1, 2, 3)]
    return peers


def net_kernel(
    x_ref, wn_hbm, steps_ref, bg_ref, be_hbm, bc_ref, br_hbm, bt_ref, bn_ref, fg_ref, fe_hbm, fc_ref, fr_hbm,
    walk_ref, ge_ref, gr_ref,
    be, br, fe, fr, bca, fca, wn, xt, u, st, acc, ab, own, pfs, pfr, flow, m0, m1, m2, m3, mf, wx,
    err, normh, act_ref, hg_ref, hs, pn, ph,
    gy_r, gz_r, r1y_r, r1z_r, ay_r, az_r, r2y_r, r2z_r, b_r, s_r, r3_r,
    gy_e, gz_e, r1y_e, r1z_e, ay_e, az_e, r2_e,
    load_sem, cs, cr, fs, fr_sem, ms, mr, gs, gr,
):
    z, l, y, h, c = place()
    core_dev = device(z, l, y, h, 1 - c)
    far_dev = device(z, l, y, 1 - h, c)
    pair_dev = device(z, 1 - l, y, h, c)
    cut_dev = device(z, 1 - l, y, 1 - h, c)
    share = pl.ds(pl.multiple_of(c * 128, 128), 128)
    other = pl.ds(pl.multiple_of((1 - c) * 128, 128), 128)

    near_cols = pl.ds(pl.multiple_of(h * 1024, 1024), 1024)
    far_cols = pl.ds(pl.multiple_of((1 - h) * 1024, 1024), 1024)

    def load(i):
        src, dst = (
            (be_hbm, be.at[c]), (br_hbm, br.at[c]), (fe_hbm, fe.at[c]), (fr_hbm, fr.at[c]),
            (wn_hbm.at[:, share], wn.at[c]),
        )[i]
        return pltpu.make_async_copy(src, dst, load_sem.at[i])

    def cross(i):
        src, dst = (
            (be_hbm, be.at[c]), (br_hbm.at[:, far_cols], br.at[c, :, far_cols]),
            (fe_hbm, fe.at[c]), (fr_hbm, fr.at[c]),
            (wn_hbm.at[:, other], wn.at[c]),
            (x_ref.at[other], xt.at[c]),
            (bca.at[c], bca.at[c]), (fca.at[c], fca.at[c]),
            (m3.at[pl.ds(2 * (1 - c), 2)], mf.at[c]),
            (st.at[pl.ds(2 * (1 - c), 2)], wx),
            (ab.at[1 - c], act_ref.at[share]),
            (normh.at[:, share], normh.at[:, share]),
            (hs, hg_ref.at[share]),
            (br_hbm.at[:, near_cols], br.at[c, :, near_cols]),
        )[i]
        return remote(src, dst, cs.at[i], cr.at[i], core_dev)

    def cross_err(j, i):
        return remote(err.at[j, share], err.at[j, share], cs.at[14 + i], cr.at[14 + i], core_dev)

    def gather(i):
        return remote(u.at[4 * h + i], u.at[4 * h + i], fs.at[i], fr_sem.at[i], far_dev)

    def reduce(i):
        return remote(pfs.at[i], pfr.at[i], fs.at[4 + i], fr_sem.at[4 + i], far_dev)

    def gather_err(i):
        j = 4 * h + i
        return remote(err.at[j, share], err.at[j, share], fs.at[8 + i], fr_sem.at[8 + i], far_dev)

    for i in (0, 1, 4):
        load(i).start()
    arrived = greet([core_dev, far_dev, cut_dev] + batch_peers(z, l, y, h, c))
    bca[c] = bc_ref[...]
    fca[c] = fc_ref[...]
    for i in range(2):
        u[4 * h + 2 * c + i] = x_ref[share, 256 * i : 256 * (i + 1)]
    xt[c] = x_ref[share]
    arrived()
    cross(5).start()
    for i in range(2):
        gather(2 * c + i).start()
    cross(6).start()
    cross(0).start()
    cross(7).start()
    cross(5).wait()
    for i in range(2):
        u[4 * h + 2 * (1 - c) + i] = xt[1 - c, :, 256 * i : 256 * (i + 1)]
        gather(2 * (1 - c) + i).start()
    cross(1).start()
    cross(13).start()
    cross(4).start()
    for i in range(4):
        st[i] = u[4 * h + i].astype(F32)

    for s in range(2):
        noise = bn_ref[128 * s : 128 * (s + 1)].astype(F32).reshape(16, 8, 512)
        times = jnp.transpose(jnp.broadcast_to(bt_ref[s : s + 1, :], (128, 128)))
        high = times.astype(BF16).astype(F32)
        low = times - high
        packed = jnp.concatenate([noise[:, :, :256], noise[:, :, 256:]], axis=1)
        clocks = jnp.concatenate([high.reshape(16, 8, 128), low.reshape(16, 8, 128)], axis=1)
        m0[2 * s : 2 * s + 2] = (
            jnp.concatenate([packed, clocks], axis=2).astype(BF16).reshape(2, 2, 4, 16, 384)
        )

    def swap_l():
        return remote(m0.at[:, 1 - l], m1.at[:, l], ms.at[0], mr.at[0], pair_dev)

    def swap_y(d):
        to = (y + d) % 4
        return remote(m1.at[:, :, to], m2.at[:, :, y], ms.at[d], mr.at[d], device(z, l, to, h, c))

    def swap_z(d):
        to = (z + d) % 4
        return remote(m2.at[to], m3.at[z], ms.at[3 + d], mr.at[3 + d], device(to, l, y, h, c))

    swap_l().start()
    m1[:, l] = m0[:, l]

    def scaled(j, gain_ref):
        rows = u[j].astype(F32)
        return jnp.sum(rows * rows, axis=1, keepdims=True), (rows * gain_ref[j]).astype(BF16)

    def expand(gain_ref, weights, finish):
        squares = jnp.zeros((ROWS, 1), F32)
        near = []
        for i in range(4):
            square, part = scaled(4 * h + i, gain_ref)
            squares += square
            near.append(part)
        near = jnp.concatenate(near, axis=1)
        near_rows = pl.ds(pl.multiple_of(h * 1024, 1024), 1024)
        for q in range(2):
            for n in range(4):
                cols = slice(256 * n, 256 * (n + 1))
                acc[q, :, cols] = jnp.dot(near, weights[q, near_rows, cols], preferred_element_type=F32)
        for i in range(4):
            gather(i).wait_recv()
            j = 4 * (1 - h) + i
            square, part = scaled(j, gain_ref)
            squares += square
            far_rows = pl.ds(pl.multiple_of(j * 256, 256), 256)
            if i == 3:
                factor = lax.rsqrt(squares * (1.0 / 2048.0) + EPSILON)
            for q in range(2):
                for n in range(4):
                    cols = slice(256 * n, 256 * (n + 1))
                    total = acc[q, :, cols] + jnp.dot(part, weights[q, far_rows, cols], preferred_element_type=F32)
                    if i < 3:
                        acc[q, :, cols] = total
                    else:
                        finish(q, cols, total * factor)
        return factor

    def contract(weights, j):
        cols = pl.ds(pl.multiple_of(j * 256, 256), 256)
        return jnp.dot(ab[0], weights[0, :, cols], preferred_element_type=F32) + jnp.dot(
            ab[1], weights[1, :, cols], preferred_element_type=F32
        )

    def reduce_start(weights, between=lambda: None):
        for i in range(4):
            pfs[i] = contract(weights, 4 * (1 - h) + i).astype(BF16)
            reduce(i).start()
        between()
        for i in range(4):
            own[i] = contract(weights, 4 * h + i)

    def reduce_wait(i):
        reduce(i).wait()
        return own[i] + pfr[i].astype(F32)

    for i in (0, 1, 4):
        load(i).wait()
    cross(0).wait()
    cross(6).wait()
    cross(7).wait()

    def step(k, clock):
        width = steps_ref[k]

        def finish(q, cols, product):
            hidden = product + clock * bca[q, :, cols]
            ab[q, :, cols] = (hidden * jax.nn.sigmoid(hidden)).astype(BF16)

        expand(bg_ref, be, finish)

        @pl.when(k == 0)
        def _():
            cross(1).wait()

        def rest():
            @pl.when(k == 0)
            def _():
                cross(13).wait()

        reduce_start(br, rest)

        @pl.when(k == 0)
        def _():
            cross(4).wait()
            for i in (2, 3):
                load(i).start()
            cross(2).start()
            swap_l().wait()
            for d in (1, 2, 3):
                swap_y(d).start()
            m2[:, :, y] = m1[:, :, y]

        @pl.when(k == 1)
        def _():
            cross(3).start()
            for d in (1, 2, 3):
                swap_y(d).wait()
            for d in (1, 2, 3):
                swap_z(d).start()
            m3[z] = m2[z]

        @pl.when(k == 2)
        def _():
            for d in (1, 2, 3):
                swap_z(d).wait()
            cross(8).start()
            mf[c] = m3[pl.ds(2 * c, 2)]

        @pl.when(k == 3)
        def _():
            cross(8).wait()

        spread = jnp.sqrt(jnp.full((1, 256), width, F32)) * NOISE_LEVEL
        for i in range(4):
            q, cols = i // 2, slice(256 * (i % 2), 256 * (i % 2) + 256)
            state = st[i] - width * reduce_wait(i) + spread * wn[q, k, :, cols].astype(F32)
            st[i] = state
            gather(i).wait_send()

            @pl.when(k != 3)
            def _():
                u[4 * h + i] = state.astype(BF16)

            @pl.when(k == 3)
            def _():
                message = mf[q].reshape(16, 16, 384).astype(F32)
                half = slice(8 * (i % 2), 8 * (i % 2) + 8)
                noise = message[:, half, :256].reshape(ROWS, 256)
                times = (message[:, :8, 256:] + message[:, 8:, 256:]).reshape(ROWS, 128)
                times = jnp.concatenate([times] * 2, axis=1)
                start = state.astype(BF16).astype(F32)
                end = xt[q, :, cols].astype(F32)
                mixed = (1.0 - times) * start + times * end + jnp.sqrt(times * (1.0 - times)) * NOISE_LEVEL * noise
                flow[i] = (end - mixed) / (1.0 - times)
                u[4 * h + i] = mixed.astype(BF16)

            gather(i).start()
        return clock - width

    lax.fori_loop(0, 4, step, jnp.float32(1.0))

    for i in (2, 3):
        load(i).wait()
        cross(i).wait()
    cross(9).start()
    message = mf[0].reshape(16, 16, 384)[:, :, 256:].astype(F32)
    times = (message[:, :8] + message[:, 8:]).reshape(ROWS, 128)
    times = jnp.concatenate([times] * 2, axis=1)

    def finish_fore(q, cols, product):
        hidden = product + times * fca[q, :, cols]
        acc[q, :, cols] = hidden
        ab[q, :, cols] = (hidden * jax.nn.sigmoid(hidden)).astype(BF16)

    factor = expand(fg_ref, fe, finish_fore)
    reduce_start(fr)
    act_ref[share] = ab[c]
    cross(10).start()
    for j in range(8):
        normh[j % 2, share, 256 * (j // 2) : 256 * (j // 2 + 1)] = (
            u[j].astype(F32) * factor * fg_ref[j]
        ).astype(BF16)
    cross(11).start()
    cross(9).wait()
    for i in range(2):
        walk_ref[share, 256 * i : 256 * (i + 1)] = st[2 * c + i]
        walk_ref[other, 256 * i : 256 * (i + 1)] = wx[i]
    scale = 1.0 / (8192.0**0.5)
    for i in range(4):
        j = 4 * h + i
        err[j, share] = ((reduce_wait(i) - flow[i]) * scale).astype(BF16)
        gather_err(i).start()
        cross_err(j, i).start()
    for i in range(4):
        gather(i).wait_send()
    cross(10).wait()
    cross(11).wait()

    def pair_normed(i):
        part = pl.ds(pl.multiple_of(c * 128 + 64 * i, 64), 64)
        dev = pair_dev if i == 0 else cut_dev
        return remote(normh.at[1 - l, part], pn.at[part], gs.at[26 + 4 * i], gr.at[26 + 4 * i], dev)

    def ydev(d):
        return device(z, l, (y + d) % 4, h, c)

    def zdev(d):
        return device((z + d) % 4, l, y, h, c)

    def pair_forward():
        return remote(pn.at[share], pn.at[share], gs.at[27], gr.at[27], core_dev)

    def pair_grad(s):
        part = share if s == 0 else other
        return remote(hg_ref.at[part], ph.at[part], gs.at[28 + s], gr.at[28 + s], pair_dev)

    def r_first_y(d):
        return remote(gy_r.at[:, :, (y + d) % 4], r1y_r.at[d - 1], gs.at[d - 1], gr.at[d - 1], ydev(d))

    def r_first_z(d):
        return remote(gz_r.at[(z + d) % 4], r1z_r.at[d - 1], gs.at[2 + d], gr.at[2 + d], zdev(d))

    def r_second_y(d):
        return remote(ay_r.at[(z + d) % 4], r2y_r.at[d - 1], gs.at[5 + d], gr.at[5 + d], zdev(d))

    def r_second_z(d):
        return remote(az_r.at[:, (y + d) % 4], r2z_r.at[d - 1], gs.at[8 + d], gr.at[8 + d], ydev(d))

    parts_r = (slice(0, WIDE), slice(WIDE, WIDE + NARROW))

    def r_third(i):
        cols = parts_r[i]
        return remote(s_r.at[:, cols], r3_r.at[:, cols], gs.at[12 + i], gr.at[12 + i], pair_dev)

    def e_first_y(d):
        return remote(gy_e.at[:, (y + d) % 4], r1y_e.at[d - 1], gs.at[13 + d], gr.at[13 + d], ydev(d))

    def e_first_z(d):
        return remote(gz_e.at[(z + d) % 4], r1z_e.at[d - 1], gs.at[16 + d], gr.at[16 + d], zdev(d))

    def e_second_y(d):
        return remote(ay_e.at[(z + d) % 4], r2_e.at[0, d - 1], gs.at[19 + d], gr.at[19 + d], zdev(d))

    def e_second_z(d):
        return remote(az_e.at[(y + d) % 4], r2_e.at[1, d - 1], gs.at[22 + d], gr.at[22 + d], ydev(d))

    def outer(left, right):
        return lax.dot_general(left, right, (((0,), (0,)), ((), ())), preferred_element_type=F32)

    def make_r(to):
        for i in range(2):
            part = outer(err[2 * to + i], act_ref[...]).astype(BF16)
            gy_r[to, i] = part[:, :WIDE].reshape(4, 64, WIDE)
            gz_r[to, i] = part[:, WIDE:].reshape(4, 64, NARROW)
            for d in (1, 2, 3):
                dst = (y + d) % 4
                remote(
                    gy_r.at[to, i, dst], r1y_r.at[d - 1, to, i], gs.at[d - 1], gr.at[d - 1], ydev(d)
                ).start()
        for d in (1, 2, 3):

            @pl.when(to == (z + d) % 4)
            def _():
                r_first_z(d).start()

    for i in range(2):
        pair_normed(i).start()
    for half in range(2):
        for i in range(2):
            cross_err(4 * h + 2 * half + i, 2 * half + i).wait_recv()
        make_r(2 * h + half)
    for i in range(4):
        gather_err(i).wait_recv()
        cross_err(4 * (1 - h) + i, 4 + i).start()
    rows_err = jnp.concatenate([err[j, share] for j in range(8)], axis=1)
    for k in range(2):
        q = c if k == 0 else 1 - c
        for n in range(4):
            cols = slice(256 * n, 256 * (n + 1))
            back = lax.dot_general(
                rows_err, fr[q, cols, :], (((1,), (1,)), ((), ())), preferred_element_type=F32
            )
            hidden = acc[q, :, cols]
            sig = jax.nn.sigmoid(hidden)
            value = (back * (sig * (1.0 + hidden * (1.0 - sig)))).astype(BF16)
            if k == 0:
                hg_ref[share, cols] = value
            else:
                hs[:, cols] = value
        if k == 0:
            pair_grad(0).start()
        else:
            cross(12).start()
    for half in range(2):
        for i in range(2):
            cross_err(4 * (1 - h) + 2 * half + i, 4 + 2 * half + i).wait_recv()
        make_r(2 * (1 - h) + half)
        if half == 0:
            cross(12).wait()
            pair_grad(1).start()
    for i in range(4):
        gather_err(i).wait_send()
        cross_err(4 * h + i, i).wait_send()
        cross_err(4 * (1 - h) + i, 4 + i).wait_send()

    pair_normed(0).wait()
    pair_normed(1).wait()
    pair_forward().start()
    pair_forward().wait()
    for s in range(2):
        pair_grad(s).wait()

    def make_e(j, _):
        to = (z + 1 + j) % 4
        column = pl.ds(pl.multiple_of(to * 256, 256), 256)
        part = (outer(normh[l, :, column], hg_ref[...]) + outer(pn[:, column], ph[...])).astype(BF16)
        gy_e[to] = part[:, :512].reshape(4, 64, 512)
        gz_e[to] = part[:, 512:].reshape(4, 64, 512)
        for d in (1, 2, 3):
            dst = (y + d) % 4
            remote(
                gy_e.at[to, dst], r1y_e.at[d - 1, to], gs.at[13 + d], gr.at[13 + d], ydev(d)
            ).start()
        return 0

    for d in (1, 2, 3):
        lax.fori_loop(d - 1, d, make_e, 0)
        e_first_z(d).start()
    lax.fori_loop(3, 4, make_e, 0)

    for d in (1, 2, 3):
        r_first_y(d).wait()

    def add_ry(i, _):
        total = gy_r[i, :, y].astype(F32) + sum(r1y_r[d, i].astype(F32) for d in range(3))
        ay_r[i] = total.astype(BF16)
        return 0

    lax.fori_loop(0, 4, add_ry, 0)
    for d in (1, 2, 3):
        r_second_y(d).start()
    for d in (1, 2, 3):
        r_first_z(d).wait()

    def add_rz(i, _):
        total = gz_r[z, :, i].astype(F32) + sum(r1z_r[d, :, i].astype(F32) for d in range(3))
        az_r[:, i] = total.astype(BF16)
        return 0

    lax.fori_loop(0, 4, add_rz, 0)
    for d in (1, 2, 3):
        r_second_z(d).start()

    def finish_r(i):
        for d in (1, 2, 3):
            (r_second_y(d) if i == 0 else r_second_z(d)).wait()

        def own(side):
            return ay_r[z, side] if i == 0 else az_r[side, y]

        landed = r2y_r if i == 0 else r2z_r
        s_r[:, parts_r[i]] = (
            own(1 - l).astype(F32) + sum(landed[d, 1 - l].astype(F32) for d in range(3))
        ).astype(BF16)
        r_third(i).start()
        b_r[:, parts_r[i]] = own(l).astype(F32) + sum(landed[d, l].astype(F32) for d in range(3))

    finish_r(0)
    finish_r(1)

    for d in (1, 2, 3):
        e_first_y(d).wait()

    def add_ey(i, _):
        total = gy_e[i, y].astype(F32) + sum(r1y_e[d, i].astype(F32) for d in range(3))
        ay_e[i] = total.astype(BF16)
        return 0

    lax.fori_loop(0, 4, add_ey, 0)
    for d in (1, 2, 3):
        e_second_y(d).start()
    for d in (1, 2, 3):
        e_first_z(d).wait()

    def add_ez(i, _):
        total = gz_e[z, i].astype(F32) + sum(r1z_e[d, i].astype(F32) for d in range(3))
        az_e[i] = total.astype(BF16)
        return 0

    lax.fori_loop(0, 4, add_ez, 0)
    for d in (1, 2, 3):
        e_second_z(d).start()
    for i in range(2):
        r_third(i).wait()
        gr_ref[:, parts_r[i]] = b_r[:, parts_r[i]] + r3_r[:, parts_r[i]].astype(F32)
    for i in range(2):
        for d in (1, 2, 3):
            (e_second_y(d) if i == 0 else e_second_z(d)).wait()
        mine = ay_e[z] if i == 0 else az_e[y]
        ge_ref[:, 512 * i : 512 * (i + 1)] = mine.astype(F32) + sum(r2_e[i, d].astype(F32) for d in range(3))


def copy_kernel(a_in, b_in, c_in, a_out, b_out, c_out, a_mid, b_mid, c_mid, sems):
    trios = ((a_in, a_mid, a_out), (b_in, b_mid, b_out), (c_in, c_mid, c_out))
    into = [pltpu.make_async_copy(src, mid, sems.at[0, i]) for i, (src, mid, dst) in enumerate(trios)]
    out = [pltpu.make_async_copy(mid, dst, sems.at[1, i]) for i, (src, mid, dst) in enumerate(trios)]
    for copy in into:
        copy.start()
    for first, second in zip(into, out):
        first.wait()
        second.start()
    for copy in out:
        copy.wait()


def body(
    target_latents, walk_noise, step_sizes, back_gain, back_expand, back_clock, back_reduce,
    bridge_times, bridge_noise, fore_gain, fore_expand, fore_clock, fore_reduce,
):
    vmem = pl.BlockSpec(memory_space=pltpu.VMEM)
    smem = pl.BlockSpec(memory_space=pltpu.SMEM)
    hbm = pl.BlockSpec(memory_space=pl.ANY)
    dma = pltpu.SemaphoreType.DMA
    sds = jax.ShapeDtypeStruct
    R = ROWS
    outs = pl.pallas_call(
        net_kernel,
        out_shape=(sds((256, 512), F32), sds((64, 1024), F32), sds((64, 1024), F32)),
        in_specs=[vmem, hbm, smem, vmem, hbm, vmem, hbm, vmem, vmem, vmem, hbm, vmem, hbm],
        out_specs=(vmem,) * 3,
        scratch_shapes=[
            pltpu.VMEM((2, 2048, 1024), BF16), pltpu.VMEM((2, 1024, 2048), BF16),
            pltpu.VMEM((2, 2048, 1024), BF16), pltpu.VMEM((2, 1024, 2048), BF16),
            pltpu.VMEM((2, 1, 1024), F32), pltpu.VMEM((2, 1, 1024), F32),
            pltpu.VMEM((2, 4, R, 512), BF16), pltpu.VMEM((2, R, 512), BF16),
            pltpu.VMEM((8, R, 256), BF16), pltpu.VMEM((4, R, 256), F32),
            pltpu.VMEM((2, R, 1024), F32), pltpu.VMEM((2, R, 1024), BF16),
            pltpu.VMEM((4, R, 256), F32), pltpu.VMEM((4, R, 256), BF16), pltpu.VMEM((4, R, 256), BF16),
            pltpu.VMEM((4, R, 256), F32),
        ]
        + [pltpu.VMEM((4, 2, 4, 16, 384), BF16)] * 4
        + [
            pltpu.VMEM((2, 2, 2, 4, 16, 384), BF16), pltpu.VMEM((2, R, 256), F32),
            pltpu.VMEM((8, 256, 256), BF16), pltpu.VMEM((2, 256, 1024), BF16),
            pltpu.VMEM((256, 1024), BF16), pltpu.VMEM((256, 1024), BF16), pltpu.VMEM((R, 1024), BF16),
            pltpu.VMEM((256, 1024), BF16), pltpu.VMEM((256, 1024), BF16),
            pltpu.VMEM((4, 2, 4, 64, WIDE), BF16), pltpu.VMEM((4, 2, 4, 64, NARROW), BF16),
            pltpu.VMEM((3, 4, 2, 64, WIDE), BF16), pltpu.VMEM((3, 2, 4, 64, NARROW), BF16),
            pltpu.VMEM((4, 2, 64, WIDE), BF16), pltpu.VMEM((2, 4, 64, NARROW), BF16),
            pltpu.VMEM((3, 2, 64, WIDE), BF16), pltpu.VMEM((3, 2, 64, NARROW), BF16),
            pltpu.VMEM((64, 1024), F32), pltpu.VMEM((64, 1024), BF16), pltpu.VMEM((64, 1024), BF16),
            pltpu.VMEM((4, 4, 64, 512), BF16), pltpu.VMEM((4, 4, 64, 512), BF16),
            pltpu.VMEM((3, 4, 64, 512), BF16), pltpu.VMEM((3, 4, 64, 512), BF16),
            pltpu.VMEM((4, 64, 512), BF16), pltpu.VMEM((4, 64, 512), BF16),
            pltpu.VMEM((2, 3, 64, 512), BF16),
        ]
        + [dma((5,)), dma((22,)), dma((22,)), dma((12,)), dma((12,)), dma((7,)), dma((7,)), dma((31,)), dma((31,))],
        compiler_params=pltpu.CompilerParams(
            collective_id=0, has_side_effects=True, vmem_limit_bytes=62 * 2**20
        ),
        name="net",
    )(
        target_latents, walk_noise, step_sizes, back_gain.reshape(8, 1, 256), back_expand,
        back_clock.reshape(1, 1024), back_reduce, bridge_times.reshape(2, 128), bridge_noise,
        fore_gain.reshape(8, 1, 256), fore_expand, fore_clock.reshape(1, 1024), fore_reduce,
    )
    return pl.pallas_call(
        copy_kernel,
        out_shape=tuple(sds(o.shape, o.dtype) for o in outs),
        in_specs=[hbm] * 3,
        out_specs=(hbm,) * 3,
        scratch_shapes=[pltpu.VMEM(o.shape, o.dtype) for o in outs] + [dma((2, 3))],
        name="place_outputs",
    )(*outs)


def solution(mesh):
    placed = (
        P("batch", "tensor"), P(None, "batch", "tensor"), P(), P(), P(None, "tensor"), P("tensor"),
        P("tensor", None), P("batch"), P("batch", "tensor"), P(), P(None, "tensor"), P("tensor"),
        P("tensor", None),
    )
    return jax.shard_map(
        body, mesh=mesh, in_specs=placed,
        out_specs=(P("batch", "tensor"), P("batch", "tensor"), P("batch", "tensor")), check_vma=False,
    )
```

```python
import jax
import jax.numpy as jnp
from jax import lax
from jax.experimental import pallas as pl
from jax.experimental.pallas import tpu as pltpu
from jax.sharding import PartitionSpec as P

NOISE_LEVEL = 0.5
EPSILON = 1e-06
MESH = pl.DeviceIdType.MESH
F32 = jnp.float32
BF16 = jnp.bfloat16
ROWS = 128
WIDE = 640
NARROW = 384


def place():
    b = lax.axis_index("batch")
    t = lax.axis_index("tensor")
    return b // 8, (b // 4) % 2, b % 4, t // 2, t % 2


def device(z, l, y, h, c):
    return (z * 8 + l * 4 + y, h * 2 + c)


def remote(src, dst, send_sem, recv_sem, dev):
    return pltpu.make_async_remote_copy(
        src_ref=src, dst_ref=dst, send_sem=send_sem, recv_sem=recv_sem, device_id=dev, device_id_type=MESH
    )


def greet(devices):
    barrier = pltpu.get_barrier_semaphore()
    for dev in devices:
        pl.semaphore_signal(barrier, inc=1, device_id=dev, device_id_type=MESH)
    return lambda: pl.semaphore_wait(barrier, len(devices))


def batch_peers(z, l, y, h, c):
    peers = [device(z, 1 - l, y, h, c)]
    peers += [device(z, l, (y + d) % 4, h, c) for d in (1, 2, 3)]
    peers += [device((z + d) % 4, l, y, h, c) for d in (1, 2, 3)]
    return peers


def net_kernel(
    x_ref, wn_hbm, steps_ref, bg_ref, be_hbm, bc_ref, br_hbm, bt_ref, bn_ref, fg_ref, fe_hbm, fc_ref, fr_hbm,
    walk_ref, ge_ref, gr_ref,
    be, br, fe, fr, bca, fca, wn, xt, u, st, acc, ab, own, pfs, pfr, flow, m0, m1, m2, m3, mf, wx,
    err, normh, act_ref, hg_ref, hs, pn, ph,
    gy_r, gz_r, r1y_r, r1z_r, ay_r, az_r, r2y_r, r2z_r, b_r, s_r, r3_r,
    gy_e, gz_e, r1y_e, r1z_e, ay_e, az_e, r2_e,
    load_sem, cs, cr, fs, fr_sem, ms, mr, gs, gr,
):
    z, l, y, h, c = place()
    core_dev = device(z, l, y, h, 1 - c)
    far_dev = device(z, l, y, 1 - h, c)
    pair_dev = device(z, 1 - l, y, h, c)
    cut_dev = device(z, 1 - l, y, 1 - h, c)
    share = pl.ds(pl.multiple_of(c * 128, 128), 128)
    other = pl.ds(pl.multiple_of((1 - c) * 128, 128), 128)

    near_cols = pl.ds(pl.multiple_of(h * 1024, 1024), 1024)
    far_cols = pl.ds(pl.multiple_of((1 - h) * 1024, 1024), 1024)

    def load(i):
        src, dst = (
            (be_hbm, be.at[c]), (br_hbm, br.at[c]), (fe_hbm, fe.at[c]), (fr_hbm, fr.at[c]),
            (wn_hbm.at[:, share], wn.at[c]),
        )[i]
        return pltpu.make_async_copy(src, dst, load_sem.at[i])

    def cross(i):
        src, dst = (
            (be_hbm, be.at[c]), (br_hbm.at[:, far_cols], br.at[c, :, far_cols]),
            (fe_hbm, fe.at[c]), (fr_hbm, fr.at[c]),
            (wn_hbm.at[:, other], wn.at[c]),
            (x_ref.at[other], xt.at[c]),
            (bca.at[c], bca.at[c]), (fca.at[c], fca.at[c]),
            (m3.at[pl.ds(2 * (1 - c), 2)], mf.at[c]),
            (st.at[pl.ds(2 * (1 - c), 2)], wx),
            (ab.at[1 - c], act_ref.at[share]),
            (normh.at[:, share], normh.at[:, share]),
            (hs, hg_ref.at[share]),
            (br_hbm.at[:, near_cols], br.at[c, :, near_cols]),
        )[i]
        return remote(src, dst, cs.at[i], cr.at[i], core_dev)

    def cross_err(j, i):
        return remote(err.at[j, share], err.at[j, share], cs.at[14 + i], cr.at[14 + i], core_dev)

    def gather(i):
        return remote(u.at[4 * h + i], u.at[4 * h + i], fs.at[i], fr_sem.at[i], far_dev)

    def reduce(i):
        return remote(pfs.at[i], pfr.at[i], fs.at[4 + i], fr_sem.at[4 + i], far_dev)

    def gather_err(i):
        j = 4 * h + i
        return remote(err.at[j, share], err.at[j, share], fs.at[8 + i], fr_sem.at[8 + i], far_dev)

    for i in (0, 1, 4):
        load(i).start()
    arrived = greet([core_dev, far_dev, cut_dev] + batch_peers(z, l, y, h, c))
    bca[c] = bc_ref[...]
    fca[c] = fc_ref[...]
    for i in range(2):
        u[4 * h + 2 * c + i] = x_ref[share, 256 * i : 256 * (i + 1)]
    xt[c] = x_ref[share]
    arrived()
    cross(5).start()
    for i in range(2):
        gather(2 * c + i).start()
    cross(6).start()
    cross(0).start()
    cross(7).start()
    cross(5).wait()
    for i in range(2):
        u[4 * h + 2 * (1 - c) + i] = xt[1 - c, :, 256 * i : 256 * (i + 1)]
        gather(2 * (1 - c) + i).start()
    cross(1).start()
    cross(13).start()
    cross(4).start()
    for i in range(4):
        st[i] = u[4 * h + i].astype(F32)

    for s in range(2):
        noise = bn_ref[128 * s : 128 * (s + 1)].astype(F32).reshape(16, 8, 512)
        times = jnp.transpose(jnp.broadcast_to(bt_ref[s : s + 1, :], (128, 128)))
        high = times.astype(BF16).astype(F32)
        low = times - high
        packed = jnp.concatenate([noise[:, :, :256], noise[:, :, 256:]], axis=1)
        clocks = jnp.concatenate([high.reshape(16, 8, 128), low.reshape(16, 8, 128)], axis=1)
        m0[2 * s : 2 * s + 2] = (
            jnp.concatenate([packed, clocks], axis=2).astype(BF16).reshape(2, 2, 4, 16, 384)
        )

    def swap_l():
        return remote(m0.at[:, 1 - l], m1.at[:, l], ms.at[0], mr.at[0], pair_dev)

    def swap_y(d):
        to = (y + d) % 4
        return remote(m1.at[:, :, to], m2.at[:, :, y], ms.at[d], mr.at[d], device(z, l, to, h, c))

    def swap_z(d):
        to = (z + d) % 4
        return remote(m2.at[to], m3.at[z], ms.at[3 + d], mr.at[3 + d], device(to, l, y, h, c))

    swap_l().start()
    m1[:, l] = m0[:, l]

    def scaled(j, gain_ref):
        rows = u[j].astype(F32)
        return jnp.sum(rows * rows, axis=1, keepdims=True), (rows * gain_ref[j]).astype(BF16)

    def expand(gain_ref, weights, finish):
        squares = jnp.zeros((ROWS, 1), F32)
        near = []
        for i in range(4):
            square, part = scaled(4 * h + i, gain_ref)
            squares += square
            near.append(part)
        near = jnp.concatenate(near, axis=1)
        near_rows = pl.ds(pl.multiple_of(h * 1024, 1024), 1024)
        for q in range(2):
            for n in range(4):
                cols = slice(256 * n, 256 * (n + 1))
                acc[q, :, cols] = jnp.dot(near, weights[q, near_rows, cols], preferred_element_type=F32)
        for i in range(4):
            gather(i).wait_recv()
            j = 4 * (1 - h) + i
            square, part = scaled(j, gain_ref)
            squares += square
            far_rows = pl.ds(pl.multiple_of(j * 256, 256), 256)
            if i == 3:
                factor = lax.rsqrt(squares * (1.0 / 2048.0) + EPSILON)
            for q in range(2):
                for n in range(4):
                    cols = slice(256 * n, 256 * (n + 1))
                    total = acc[q, :, cols] + jnp.dot(part, weights[q, far_rows, cols], preferred_element_type=F32)
                    if i < 3:
                        acc[q, :, cols] = total
                    else:
                        finish(q, cols, total * factor)
        return factor

    def contract(weights, j):
        cols = pl.ds(pl.multiple_of(j * 256, 256), 256)
        return jnp.dot(ab[0], weights[0, :, cols], preferred_element_type=F32) + jnp.dot(
            ab[1], weights[1, :, cols], preferred_element_type=F32
        )

    def reduce_start(weights, between=lambda: None):
        for i in range(4):
            pfs[i] = contract(weights, 4 * (1 - h) + i).astype(BF16)
            reduce(i).start()
        between()
        for i in range(4):
            own[i] = contract(weights, 4 * h + i)

    def reduce_wait(i):
        reduce(i).wait()
        return own[i] + pfr[i].astype(F32)

    for i in (0, 1, 4):
        load(i).wait()
    cross(0).wait()
    cross(6).wait()
    cross(7).wait()

    def step(k, clock):
        width = steps_ref[k]

        def finish(q, cols, product):
            hidden = product + clock * bca[q, :, cols]
            ab[q, :, cols] = (hidden * jax.nn.sigmoid(hidden)).astype(BF16)

        expand(bg_ref, be, finish)

        @pl.when(k == 0)
        def _():
            cross(1).wait()

        def rest():
            @pl.when(k == 0)
            def _():
                cross(13).wait()

        reduce_start(br, rest)

        @pl.when(k == 0)
        def _():
            cross(4).wait()
            for i in (2, 3):
                load(i).start()
            cross(2).start()
            swap_l().wait()
            for d in (1, 2, 3):
                swap_y(d).start()
            m2[:, :, y] = m1[:, :, y]

        @pl.when(k == 1)
        def _():
            cross(3).start()
            for d in (1, 2, 3):
                swap_y(d).wait()
            for d in (1, 2, 3):
                swap_z(d).start()
            m3[z] = m2[z]

        @pl.when(k == 2)
        def _():
            for d in (1, 2, 3):
                swap_z(d).wait()
            cross(8).start()
            mf[c] = m3[pl.ds(2 * c, 2)]

        @pl.when(k == 3)
        def _():
            cross(8).wait()

        spread = jnp.sqrt(jnp.full((1, 256), width, F32)) * NOISE_LEVEL
        for i in range(4):
            q, cols = i // 2, slice(256 * (i % 2), 256 * (i % 2) + 256)
            state = st[i] - width * reduce_wait(i) + spread * wn[q, k, :, cols].astype(F32)
            st[i] = state
            gather(i).wait_send()

            @pl.when(k != 3)
            def _():
                u[4 * h + i] = state.astype(BF16)

            @pl.when(k == 3)
            def _():
                message = mf[q].reshape(16, 16, 384).astype(F32)
                half = slice(8 * (i % 2), 8 * (i % 2) + 8)
                noise = message[:, half, :256].reshape(ROWS, 256)
                times = (message[:, :8, 256:] + message[:, 8:, 256:]).reshape(ROWS, 128)
                times = jnp.concatenate([times] * 2, axis=1)
                start = state.astype(BF16).astype(F32)
                end = xt[q, :, cols].astype(F32)
                mixed = (1.0 - times) * start + times * end + jnp.sqrt(times * (1.0 - times)) * NOISE_LEVEL * noise
                flow[i] = (end - mixed) / (1.0 - times)
                u[4 * h + i] = mixed.astype(BF16)

            gather(i).start()
        return clock - width

    lax.fori_loop(0, 4, step, jnp.float32(1.0))

    for i in (2, 3):
        load(i).wait()
        cross(i).wait()
    cross(9).start()
    message = mf[0].reshape(16, 16, 384)[:, :, 256:].astype(F32)
    times = (message[:, :8] + message[:, 8:]).reshape(ROWS, 128)
    times = jnp.concatenate([times] * 2, axis=1)

    def finish_fore(q, cols, product):
        hidden = product + times * fca[q, :, cols]
        acc[q, :, cols] = hidden
        ab[q, :, cols] = (hidden * jax.nn.sigmoid(hidden)).astype(BF16)

    factor = expand(fg_ref, fe, finish_fore)
    reduce_start(fr)
    act_ref[share] = ab[c]
    cross(10).start()
    for j in range(8):
        normh[j % 2, share, 256 * (j // 2) : 256 * (j // 2 + 1)] = (
            u[j].astype(F32) * factor * fg_ref[j]
        ).astype(BF16)
    cross(11).start()
    cross(9).wait()
    for i in range(2):
        walk_ref[share, 256 * i : 256 * (i + 1)] = st[2 * c + i]
        walk_ref[other, 256 * i : 256 * (i + 1)] = wx[i]
    scale = 1.0 / (8192.0**0.5)
    for i in range(4):
        j = 4 * h + i
        err[j, share] = ((reduce_wait(i) - flow[i]) * scale).astype(BF16)
        gather_err(i).start()
        cross_err(j, i).start()
    for i in range(4):
        gather(i).wait_send()
    cross(10).wait()
    cross(11).wait()

    def pair_normed(i):
        part = pl.ds(pl.multiple_of(c * 128 + 64 * i, 64), 64)
        dev = pair_dev if i == 0 else cut_dev
        return remote(normh.at[1 - l, part], pn.at[part], gs.at[26 + 4 * i], gr.at[26 + 4 * i], dev)

    def ydev(d):
        return device(z, l, (y + d) % 4, h, c)

    def zdev(d):
        return device((z + d) % 4, l, y, h, c)

    def pair_forward():
        return remote(pn.at[share], pn.at[share], gs.at[27], gr.at[27], core_dev)

    def pair_grad(s):
        part = share if s == 0 else other
        return remote(hg_ref.at[part], ph.at[part], gs.at[28 + s], gr.at[28 + s], pair_dev)

    def r_first_y(d):
        return remote(gy_r.at[:, :, (y + d) % 4], r1y_r.at[d - 1], gs.at[d - 1], gr.at[d - 1], ydev(d))

    def r_first_z(d):
        return remote(gz_r.at[(z + d) % 4], r1z_r.at[d - 1], gs.at[2 + d], gr.at[2 + d], zdev(d))

    def r_second_y(d):
        return remote(ay_r.at[(z + d) % 4], r2y_r.at[d - 1], gs.at[5 + d], gr.at[5 + d], zdev(d))

    def r_second_z(d):
        return remote(az_r.at[:, (y + d) % 4], r2z_r.at[d - 1], gs.at[8 + d], gr.at[8 + d], ydev(d))

    parts_r = (slice(0, WIDE), slice(WIDE, WIDE + NARROW))

    def r_third(i):
        cols = parts_r[i]
        return remote(s_r.at[:, cols], r3_r.at[:, cols], gs.at[12 + i], gr.at[12 + i], pair_dev)

    def e_first_y(d):
        return remote(gy_e.at[:, (y + d) % 4], r1y_e.at[d - 1], gs.at[13 + d], gr.at[13 + d], ydev(d))

    def e_first_z(d):
        return remote(gz_e.at[(z + d) % 4], r1z_e.at[d - 1], gs.at[16 + d], gr.at[16 + d], zdev(d))

    def e_second_y(d):
        return remote(ay_e.at[(z + d) % 4], r2_e.at[0, d - 1], gs.at[19 + d], gr.at[19 + d], zdev(d))

    def e_second_z(d):
        return remote(az_e.at[(y + d) % 4], r2_e.at[1, d - 1], gs.at[22 + d], gr.at[22 + d], ydev(d))

    def outer(left, right):
        return lax.dot_general(left, right, (((0,), (0,)), ((), ())), preferred_element_type=F32)

    def make_r(to):
        for i in range(2):
            part = outer(err[2 * to + i], act_ref[...]).astype(BF16)
            gy_r[to, i] = part[:, :WIDE].reshape(4, 64, WIDE)
            gz_r[to, i] = part[:, WIDE:].reshape(4, 64, NARROW)
            for d in (1, 2, 3):
                dst = (y + d) % 4
                remote(
                    gy_r.at[to, i, dst], r1y_r.at[d - 1, to, i], gs.at[d - 1], gr.at[d - 1], ydev(d)
                ).start()
        for d in (1, 2, 3):

            @pl.when(to == (z + d) % 4)
            def _():
                r_first_z(d).start()

    for i in range(2):
        pair_normed(i).start()
    for half in range(2):
        for i in range(2):
            cross_err(4 * h + 2 * half + i, 2 * half + i).wait_recv()
        make_r(2 * h + half)
    for i in range(4):
        gather_err(i).wait_recv()
        cross_err(4 * (1 - h) + i, 4 + i).start()
    for half in range(2):
        for i in range(2):
            cross_err(4 * (1 - h) + 2 * half + i, 4 + 2 * half + i).wait_recv()
        make_r(2 * (1 - h) + half)
    rows_err = jnp.concatenate([err[j, share] for j in range(8)], axis=1)
    for k in range(2):
        q = c if k == 0 else 1 - c
        for n in range(4):
            cols = slice(256 * n, 256 * (n + 1))
            back = lax.dot_general(
                rows_err, fr[q, cols, :], (((1,), (1,)), ((), ())), preferred_element_type=F32
            )
            hidden = acc[q, :, cols]
            sig = jax.nn.sigmoid(hidden)
            value = (back * (sig * (1.0 + hidden * (1.0 - sig)))).astype(BF16)
            if k == 0:
                hg_ref[share, cols] = value
            else:
                hs[:, cols] = value
        if k == 0:
            pair_grad(0).start()
        else:
            cross(12).start()
    cross(12).wait()
    pair_grad(1).start()
    for i in range(4):
        gather_err(i).wait_send()
        cross_err(4 * h + i, i).wait_send()
        cross_err(4 * (1 - h) + i, 4 + i).wait_send()

    pair_normed(0).wait()
    pair_normed(1).wait()
    pair_forward().start()
    pair_forward().wait()
    for s in range(2):
        pair_grad(s).wait()

    def make_e(j, _):
        to = (z + 1 + j) % 4
        column = pl.ds(pl.multiple_of(to * 256, 256), 256)
        part = (outer(normh[l, :, column], hg_ref[...]) + outer(pn[:, column], ph[...])).astype(BF16)
        gy_e[to] = part[:, :512].reshape(4, 64, 512)
        gz_e[to] = part[:, 512:].reshape(4, 64, 512)
        for d in (1, 2, 3):
            dst = (y + d) % 4
            remote(
                gy_e.at[to, dst], r1y_e.at[d - 1, to], gs.at[13 + d], gr.at[13 + d], ydev(d)
            ).start()
        return 0

    for d in (1, 2, 3):
        lax.fori_loop(d - 1, d, make_e, 0)
        e_first_z(d).start()
    lax.fori_loop(3, 4, make_e, 0)

    for d in (1, 2, 3):
        r_first_y(d).wait()

    def add_ry(i, _):
        total = gy_r[i, :, y].astype(F32) + sum(r1y_r[d, i].astype(F32) for d in range(3))
        ay_r[i] = total.astype(BF16)
        return 0

    lax.fori_loop(0, 4, add_ry, 0)
    for d in (1, 2, 3):
        r_second_y(d).start()
    for d in (1, 2, 3):
        r_first_z(d).wait()

    def add_rz(i, _):
        total = gz_r[z, :, i].astype(F32) + sum(r1z_r[d, :, i].astype(F32) for d in range(3))
        az_r[:, i] = total.astype(BF16)
        return 0

    lax.fori_loop(0, 4, add_rz, 0)
    for d in (1, 2, 3):
        r_second_z(d).start()

    def finish_r(i):
        for d in (1, 2, 3):
            (r_second_y(d) if i == 0 else r_second_z(d)).wait()

        def own(side):
            return ay_r[z, side] if i == 0 else az_r[side, y]

        landed = r2y_r if i == 0 else r2z_r
        s_r[:, parts_r[i]] = (
            own(1 - l).astype(F32) + sum(landed[d, 1 - l].astype(F32) for d in range(3))
        ).astype(BF16)
        r_third(i).start()
        b_r[:, parts_r[i]] = own(l).astype(F32) + sum(landed[d, l].astype(F32) for d in range(3))

    for d in (1, 2, 3):
        e_first_y(d).wait()

    def add_ey(i, _):
        total = gy_e[i, y].astype(F32) + sum(r1y_e[d, i].astype(F32) for d in range(3))
        ay_e[i] = total.astype(BF16)
        return 0

    lax.fori_loop(0, 4, add_ey, 0)
    for d in (1, 2, 3):
        e_second_y(d).start()
    for d in (1, 2, 3):
        e_first_z(d).wait()

    def add_ez(i, _):
        total = gz_e[z, i].astype(F32) + sum(r1z_e[d, i].astype(F32) for d in range(3))
        az_e[i] = total.astype(BF16)
        return 0

    lax.fori_loop(0, 4, add_ez, 0)
    for d in (1, 2, 3):
        e_second_z(d).start()
    finish_r(0)
    finish_r(1)
    for i in range(2):
        for d in (1, 2, 3):
            (e_second_y(d) if i == 0 else e_second_z(d)).wait()
        mine = ay_e[z] if i == 0 else az_e[y]
        ge_ref[:, 512 * i : 512 * (i + 1)] = mine.astype(F32) + sum(r2_e[i, d].astype(F32) for d in range(3))
    for i in range(2):
        r_third(i).wait()
        gr_ref[:, parts_r[i]] = b_r[:, parts_r[i]] + r3_r[:, parts_r[i]].astype(F32)


def copy_kernel(a_in, b_in, c_in, a_out, b_out, c_out, a_mid, b_mid, c_mid, sems):
    trios = ((a_in, a_mid, a_out), (b_in, b_mid, b_out), (c_in, c_mid, c_out))
    into = [pltpu.make_async_copy(src, mid, sems.at[0, i]) for i, (src, mid, dst) in enumerate(trios)]
    out = [pltpu.make_async_copy(mid, dst, sems.at[1, i]) for i, (src, mid, dst) in enumerate(trios)]
    for copy in into:
        copy.start()
    for first, second in zip(into, out):
        first.wait()
        second.start()
    for copy in out:
        copy.wait()


def body(
    target_latents, walk_noise, step_sizes, back_gain, back_expand, back_clock, back_reduce,
    bridge_times, bridge_noise, fore_gain, fore_expand, fore_clock, fore_reduce,
):
    vmem = pl.BlockSpec(memory_space=pltpu.VMEM)
    smem = pl.BlockSpec(memory_space=pltpu.SMEM)
    hbm = pl.BlockSpec(memory_space=pl.ANY)
    dma = pltpu.SemaphoreType.DMA
    sds = jax.ShapeDtypeStruct
    R = ROWS
    outs = pl.pallas_call(
        net_kernel,
        out_shape=(sds((256, 512), F32), sds((64, 1024), F32), sds((64, 1024), F32)),
        in_specs=[vmem, hbm, smem, vmem, hbm, vmem, hbm, vmem, vmem, vmem, hbm, vmem, hbm],
        out_specs=(vmem,) * 3,
        scratch_shapes=[
            pltpu.VMEM((2, 2048, 1024), BF16), pltpu.VMEM((2, 1024, 2048), BF16),
            pltpu.VMEM((2, 2048, 1024), BF16), pltpu.VMEM((2, 1024, 2048), BF16),
            pltpu.VMEM((2, 1, 1024), F32), pltpu.VMEM((2, 1, 1024), F32),
            pltpu.VMEM((2, 4, R, 512), BF16), pltpu.VMEM((2, R, 512), BF16),
            pltpu.VMEM((8, R, 256), BF16), pltpu.VMEM((4, R, 256), F32),
            pltpu.VMEM((2, R, 1024), F32), pltpu.VMEM((2, R, 1024), BF16),
            pltpu.VMEM((4, R, 256), F32), pltpu.VMEM((4, R, 256), BF16), pltpu.VMEM((4, R, 256), BF16),
            pltpu.VMEM((4, R, 256), F32),
        ]
        + [pltpu.VMEM((4, 2, 4, 16, 384), BF16)] * 4
        + [
            pltpu.VMEM((2, 2, 2, 4, 16, 384), BF16), pltpu.VMEM((2, R, 256), F32),
            pltpu.VMEM((8, 256, 256), BF16), pltpu.VMEM((2, 256, 1024), BF16),
            pltpu.VMEM((256, 1024), BF16), pltpu.VMEM((256, 1024), BF16), pltpu.VMEM((R, 1024), BF16),
            pltpu.VMEM((256, 1024), BF16), pltpu.VMEM((256, 1024), BF16),
            pltpu.VMEM((4, 2, 4, 64, WIDE), BF16), pltpu.VMEM((4, 2, 4, 64, NARROW), BF16),
            pltpu.VMEM((3, 4, 2, 64, WIDE), BF16), pltpu.VMEM((3, 2, 4, 64, NARROW), BF16),
            pltpu.VMEM((4, 2, 64, WIDE), BF16), pltpu.VMEM((2, 4, 64, NARROW), BF16),
            pltpu.VMEM((3, 2, 64, WIDE), BF16), pltpu.VMEM((3, 2, 64, NARROW), BF16),
            pltpu.VMEM((64, 1024), F32), pltpu.VMEM((64, 1024), BF16), pltpu.VMEM((64, 1024), BF16),
            pltpu.VMEM((4, 4, 64, 512), BF16), pltpu.VMEM((4, 4, 64, 512), BF16),
            pltpu.VMEM((3, 4, 64, 512), BF16), pltpu.VMEM((3, 4, 64, 512), BF16),
            pltpu.VMEM((4, 64, 512), BF16), pltpu.VMEM((4, 64, 512), BF16),
            pltpu.VMEM((2, 3, 64, 512), BF16),
        ]
        + [dma((5,)), dma((22,)), dma((22,)), dma((12,)), dma((12,)), dma((7,)), dma((7,)), dma((31,)), dma((31,))],
        compiler_params=pltpu.CompilerParams(
            collective_id=0, has_side_effects=True, vmem_limit_bytes=62 * 2**20
        ),
        name="net",
    )(
        target_latents, walk_noise, step_sizes, back_gain.reshape(8, 1, 256), back_expand,
        back_clock.reshape(1, 1024), back_reduce, bridge_times.reshape(2, 128), bridge_noise,
        fore_gain.reshape(8, 1, 256), fore_expand, fore_clock.reshape(1, 1024), fore_reduce,
    )
    return pl.pallas_call(
        copy_kernel,
        out_shape=tuple(sds(o.shape, o.dtype) for o in outs),
        in_specs=[hbm] * 3,
        out_specs=(hbm,) * 3,
        scratch_shapes=[pltpu.VMEM(o.shape, o.dtype) for o in outs] + [dma((2, 3))],
        name="place_outputs",
    )(*outs)


def solution(mesh):
    placed = (
        P("batch", "tensor"), P(None, "batch", "tensor"), P(), P(), P(None, "tensor"), P("tensor"),
        P("tensor", None), P("batch"), P("batch", "tensor"), P(), P(None, "tensor"), P("tensor"),
        P("tensor", None),
    )
    return jax.shard_map(
        body, mesh=mesh, in_specs=placed,
        out_specs=(P("batch", "tensor"), P("batch", "tensor"), P("batch", "tensor")), check_vma=False,
    )
```

```python
import jax
import jax.numpy as jnp
from jax import lax
from jax.experimental import pallas as pl
from jax.experimental.pallas import tpu as pltpu
from jax.sharding import PartitionSpec as P

NOISE_LEVEL = 0.5
EPSILON = 1e-06
MESH = pl.DeviceIdType.MESH
F32 = jnp.float32
BF16 = jnp.bfloat16
ROWS = 128
WIDE = 640
NARROW = 384


def place():
    b = lax.axis_index("batch")
    t = lax.axis_index("tensor")
    return b // 8, (b // 4) % 2, b % 4, t // 2, t % 2


def device(z, l, y, h, c):
    return (z * 8 + l * 4 + y, h * 2 + c)


def remote(src, dst, send_sem, recv_sem, dev):
    return pltpu.make_async_remote_copy(
        src_ref=src, dst_ref=dst, send_sem=send_sem, recv_sem=recv_sem, device_id=dev, device_id_type=MESH
    )


def greet(devices):
    barrier = pltpu.get_barrier_semaphore()
    for dev in devices:
        pl.semaphore_signal(barrier, inc=1, device_id=dev, device_id_type=MESH)
    return lambda: pl.semaphore_wait(barrier, len(devices))


def batch_peers(z, l, y, h, c):
    peers = [device(z, 1 - l, y, h, c)]
    peers += [device(z, l, (y + d) % 4, h, c) for d in (1, 2, 3)]
    peers += [device((z + d) % 4, l, y, h, c) for d in (1, 2, 3)]
    return peers


def net_kernel(
    x_ref, wn_hbm, steps_ref, bg_ref, be_hbm, bc_ref, br_hbm, bt_ref, bn_ref, fg_ref, fe_hbm, fc_ref, fr_hbm,
    walk_ref, ge_ref, gr_ref,
    be, br, fe, fr, bca, fca, wn, xt, u, st, acc, ab, own, pfs, pfr, flow, m0, m1, m2, m3, mf, wx,
    err, normh, act_ref, hg_ref, hs, pn, ph,
    gy_r, gz_r, r1y_r, r1z_r, ay_r, az_r, r2y_r, r2z_r, b_r, s_r, r3_r,
    gy_e, gz_e, r1y_e, r1z_e, ay_e, az_e, r2_e,
    load_sem, cs, cr, fs, fr_sem, ms, mr, gs, gr,
):
    z, l, y, h, c = place()
    core_dev = device(z, l, y, h, 1 - c)
    far_dev = device(z, l, y, 1 - h, c)
    pair_dev = device(z, 1 - l, y, h, c)
    cut_dev = device(z, 1 - l, y, 1 - h, c)
    share = pl.ds(pl.multiple_of(c * 128, 128), 128)
    other = pl.ds(pl.multiple_of((1 - c) * 128, 128), 128)

    near_cols = pl.ds(pl.multiple_of(h * 1024, 1024), 1024)
    far_cols = pl.ds(pl.multiple_of((1 - h) * 1024, 1024), 1024)

    def load(i):
        src, dst = (
            (be_hbm, be.at[c]), (br_hbm, br.at[c]), (fe_hbm, fe.at[c]), (fr_hbm, fr.at[c]),
            (wn_hbm.at[:, share], wn.at[c]),
        )[i]
        return pltpu.make_async_copy(src, dst, load_sem.at[i])

    def cross(i):
        src, dst = (
            (be_hbm, be.at[c]), (br_hbm.at[:, far_cols], br.at[c, :, far_cols]),
            (fe_hbm, fe.at[c]), (fr_hbm, fr.at[c]),
            (wn_hbm.at[:, other], wn.at[c]),
            (x_ref.at[other], xt.at[c]),
            (bca.at[c], bca.at[c]), (fca.at[c], fca.at[c]),
            (m3.at[pl.ds(2 * (1 - c), 2)], mf.at[c]),
            (st.at[pl.ds(2 * (1 - c), 2)], wx),
            (ab.at[1 - c], act_ref.at[share]),
            (normh.at[:, share], normh.at[:, share]),
            (hs, hg_ref.at[share]),
            (br_hbm.at[:, near_cols], br.at[c, :, near_cols]),
        )[i]
        return remote(src, dst, cs.at[i], cr.at[i], core_dev)

    def cross_err(j, i):
        return remote(err.at[j, share], err.at[j, share], cs.at[14 + i], cr.at[14 + i], core_dev)

    def gather(i):
        return remote(u.at[4 * h + i], u.at[4 * h + i], fs.at[i], fr_sem.at[i], far_dev)

    def reduce(i):
        return remote(pfs.at[i], pfr.at[i], fs.at[4 + i], fr_sem.at[4 + i], far_dev)

    def gather_err(i):
        j = 4 * h + i
        return remote(err.at[j, share], err.at[j, share], fs.at[8 + i], fr_sem.at[8 + i], far_dev)

    for i in (0, 1, 4):
        load(i).start()
    arrived = greet([core_dev, far_dev, cut_dev] + batch_peers(z, l, y, h, c))
    bca[c] = bc_ref[...]
    fca[c] = fc_ref[...]
    for i in range(2):
        u[4 * h + 2 * c + i] = x_ref[share, 256 * i : 256 * (i + 1)]
    xt[c] = x_ref[share]
    arrived()
    cross(5).start()
    for i in range(2):
        gather(2 * c + i).start()
    cross(6).start()
    cross(0).start()
    cross(7).start()
    cross(5).wait()
    for i in range(2):
        u[4 * h + 2 * (1 - c) + i] = xt[1 - c, :, 256 * i : 256 * (i + 1)]
        gather(2 * (1 - c) + i).start()
    cross(1).start()
    cross(13).start()
    cross(4).start()
    for i in range(4):
        st[i] = u[4 * h + i].astype(F32)

    for s in range(2):
        noise = bn_ref[128 * s : 128 * (s + 1)].astype(F32).reshape(16, 8, 512)
        times = jnp.transpose(jnp.broadcast_to(bt_ref[s : s + 1, :], (128, 128)))
        high = times.astype(BF16).astype(F32)
        low = times - high
        packed = jnp.concatenate([noise[:, :, :256], noise[:, :, 256:]], axis=1)
        clocks = jnp.concatenate([high.reshape(16, 8, 128), low.reshape(16, 8, 128)], axis=1)
        m0[2 * s : 2 * s + 2] = (
            jnp.concatenate([packed, clocks], axis=2).astype(BF16).reshape(2, 2, 4, 16, 384)
        )

    def swap_l():
        return remote(m0.at[:, 1 - l], m1.at[:, l], ms.at[0], mr.at[0], pair_dev)

    def swap_y(d):
        to = (y + d) % 4
        return remote(m1.at[:, :, to], m2.at[:, :, y], ms.at[d], mr.at[d], device(z, l, to, h, c))

    def swap_z(d):
        to = (z + d) % 4
        return remote(m2.at[to], m3.at[z], ms.at[3 + d], mr.at[3 + d], device(to, l, y, h, c))

    swap_l().start()
    m1[:, l] = m0[:, l]

    def scaled(j, gain_ref):
        rows = u[j].astype(F32)
        return jnp.sum(rows * rows, axis=1, keepdims=True), (rows * gain_ref[j]).astype(BF16)

    def expand(gain_ref, weights, finish):
        squares = jnp.zeros((ROWS, 1), F32)
        near = []
        for i in range(4):
            square, part = scaled(4 * h + i, gain_ref)
            squares += square
            near.append(part)
        near = jnp.concatenate(near, axis=1)
        near_rows = pl.ds(pl.multiple_of(h * 1024, 1024), 1024)
        for q in range(2):
            for n in range(4):
                cols = slice(256 * n, 256 * (n + 1))
                acc[q, :, cols] = jnp.dot(near, weights[q, near_rows, cols], preferred_element_type=F32)
        for i in range(4):
            gather(i).wait_recv()
            j = 4 * (1 - h) + i
            square, part = scaled(j, gain_ref)
            squares += square
            far_rows = pl.ds(pl.multiple_of(j * 256, 256), 256)
            if i == 3:
                factor = lax.rsqrt(squares * (1.0 / 2048.0) + EPSILON)
            for q in range(2):
                for n in range(4):
                    cols = slice(256 * n, 256 * (n + 1))
                    total = acc[q, :, cols] + jnp.dot(part, weights[q, far_rows, cols], preferred_element_type=F32)
                    if i < 3:
                        acc[q, :, cols] = total
                    else:
                        finish(q, cols, total * factor)
        return factor

    def contract(weights, j):
        cols = pl.ds(pl.multiple_of(j * 256, 256), 256)
        return jnp.dot(ab[0], weights[0, :, cols], preferred_element_type=F32) + jnp.dot(
            ab[1], weights[1, :, cols], preferred_element_type=F32
        )

    def reduce_start(weights, between=lambda: None):
        for i in range(4):
            pfs[i] = contract(weights, 4 * (1 - h) + i).astype(BF16)
            reduce(i).start()
        between()
        for i in range(4):
            own[i] = contract(weights, 4 * h + i)

    def reduce_wait(i):
        reduce(i).wait()
        return own[i] + pfr[i].astype(F32)

    for i in (0, 1, 4):
        load(i).wait()
    cross(0).wait()
    cross(6).wait()
    cross(7).wait()

    def step(k, clock):
        width = steps_ref[k]

        def finish(q, cols, product):
            hidden = product + clock * bca[q, :, cols]
            ab[q, :, cols] = (hidden * jax.nn.sigmoid(hidden)).astype(BF16)

        expand(bg_ref, be, finish)

        @pl.when(k == 0)
        def _():
            cross(1).wait()

        def rest():
            @pl.when(k == 0)
            def _():
                cross(13).wait()

        reduce_start(br, rest)

        @pl.when(k == 0)
        def _():
            cross(4).wait()
            for i in (2, 3):
                load(i).start()
            cross(2).start()
            swap_l().wait()
            for d in (1, 2, 3):
                swap_y(d).start()
            m2[:, :, y] = m1[:, :, y]

        @pl.when(k == 1)
        def _():
            cross(3).start()
            for d in (1, 2, 3):
                swap_y(d).wait()
            for d in (1, 2, 3):
                swap_z(d).start()
            m3[z] = m2[z]

        @pl.when(k == 2)
        def _():
            for d in (1, 2, 3):
                swap_z(d).wait()
            cross(8).start()
            mf[c] = m3[pl.ds(2 * c, 2)]

        @pl.when(k == 3)
        def _():
            cross(8).wait()

        spread = jnp.sqrt(jnp.full((1, 256), width, F32)) * NOISE_LEVEL
        for i in range(4):
            q, cols = i // 2, slice(256 * (i % 2), 256 * (i % 2) + 256)
            state = st[i] - width * reduce_wait(i) + spread * wn[q, k, :, cols].astype(F32)
            st[i] = state
            gather(i).wait_send()

            @pl.when(k != 3)
            def _():
                u[4 * h + i] = state.astype(BF16)

            @pl.when(k == 3)
            def _():
                message = mf[q].reshape(16, 16, 384).astype(F32)
                half = slice(8 * (i % 2), 8 * (i % 2) + 8)
                noise = message[:, half, :256].reshape(ROWS, 256)
                times = (message[:, :8, 256:] + message[:, 8:, 256:]).reshape(ROWS, 128)
                times = jnp.concatenate([times] * 2, axis=1)
                start = state.astype(BF16).astype(F32)
                end = xt[q, :, cols].astype(F32)
                mixed = (1.0 - times) * start + times * end + jnp.sqrt(times * (1.0 - times)) * NOISE_LEVEL * noise
                flow[i] = (end - mixed) / (1.0 - times)
                u[4 * h + i] = mixed.astype(BF16)

            gather(i).start()
        return clock - width

    lax.fori_loop(0, 4, step, jnp.float32(1.0))

    for i in (2, 3):
        load(i).wait()
        cross(i).wait()
    cross(9).start()
    message = mf[0].reshape(16, 16, 384)[:, :, 256:].astype(F32)
    times = (message[:, :8] + message[:, 8:]).reshape(ROWS, 128)
    times = jnp.concatenate([times] * 2, axis=1)

    def finish_fore(q, cols, product):
        hidden = product + times * fca[q, :, cols]
        acc[q, :, cols] = hidden
        ab[q, :, cols] = (hidden * jax.nn.sigmoid(hidden)).astype(BF16)

    factor = expand(fg_ref, fe, finish_fore)
    reduce_start(fr)
    act_ref[share] = ab[c]
    cross(10).start()
    for j in range(8):
        normh[j % 2, share, 256 * (j // 2) : 256 * (j // 2 + 1)] = (
            u[j].astype(F32) * factor * fg_ref[j]
        ).astype(BF16)
    cross(11).start()
    cross(9).wait()
    for i in range(2):
        walk_ref[share, 256 * i : 256 * (i + 1)] = st[2 * c + i]
        walk_ref[other, 256 * i : 256 * (i + 1)] = wx[i]
    scale = 1.0 / (8192.0**0.5)
    for i in range(4):
        j = 4 * h + i
        err[j, share] = ((reduce_wait(i) - flow[i]) * scale).astype(BF16)
        gather_err(i).start()
        cross_err(j, i).start()
    for i in range(4):
        gather(i).wait_send()
    cross(10).wait()
    cross(11).wait()

    def pair_normed(i):
        part = pl.ds(pl.multiple_of(c * 128 + 64 * i, 64), 64)
        dev = pair_dev if i == 0 else cut_dev
        return remote(normh.at[1 - l, part], pn.at[part], gs.at[26 + 4 * i], gr.at[26 + 4 * i], dev)

    def ydev(d):
        return device(z, l, (y + d) % 4, h, c)

    def zdev(d):
        return device((z + d) % 4, l, y, h, c)

    def pair_forward():
        return remote(pn.at[share], pn.at[share], gs.at[27], gr.at[27], core_dev)

    def pair_grad(s):
        part = share if s == 0 else other
        return remote(hg_ref.at[part], ph.at[part], gs.at[28 + s], gr.at[28 + s], pair_dev)

    def r_first_y(d):
        return remote(gy_r.at[:, :, (y + d) % 4], r1y_r.at[d - 1], gs.at[d - 1], gr.at[d - 1], ydev(d))

    def r_first_z(d):
        return remote(gz_r.at[(z + d) % 4], r1z_r.at[d - 1], gs.at[2 + d], gr.at[2 + d], zdev(d))

    def r_second_y(d):
        return remote(ay_r.at[(z + d) % 4], r2y_r.at[d - 1], gs.at[5 + d], gr.at[5 + d], zdev(d))

    def r_second_z(d):
        return remote(az_r.at[:, (y + d) % 4], r2z_r.at[d - 1], gs.at[8 + d], gr.at[8 + d], ydev(d))

    parts_r = (slice(0, WIDE), slice(WIDE, WIDE + NARROW))

    def r_third(i):
        cols = parts_r[i]
        return remote(s_r.at[:, cols], r3_r.at[:, cols], gs.at[12 + i], gr.at[12 + i], pair_dev)

    def e_first_y(d):
        return remote(gy_e.at[:, (y + d) % 4], r1y_e.at[d - 1], gs.at[13 + d], gr.at[13 + d], ydev(d))

    def e_first_z(d):
        return remote(gz_e.at[(z + d) % 4], r1z_e.at[d - 1], gs.at[16 + d], gr.at[16 + d], zdev(d))

    def e_second_y(d):
        return remote(ay_e.at[(z + d) % 4], r2_e.at[0, d - 1], gs.at[19 + d], gr.at[19 + d], zdev(d))

    def e_second_z(d):
        return remote(az_e.at[(y + d) % 4], r2_e.at[1, d - 1], gs.at[22 + d], gr.at[22 + d], ydev(d))

    def outer(left, right):
        return lax.dot_general(left, right, (((0,), (0,)), ((), ())), preferred_element_type=F32)

    def make_r(to):
        for i in range(2):
            part = outer(err[2 * to + i], act_ref[...]).astype(BF16)
            gy_r[to, i] = part[:, :WIDE].reshape(4, 64, WIDE)
            gz_r[to, i] = part[:, WIDE:].reshape(4, 64, NARROW)
            for d in (1, 2, 3):
                dst = (y + d) % 4
                remote(
                    gy_r.at[to, i, dst], r1y_r.at[d - 1, to, i], gs.at[d - 1], gr.at[d - 1], ydev(d)
                ).start()
        for d in (1, 2, 3):

            @pl.when(to == (z + d) % 4)
            def _():
                r_first_z(d).start()

    for half in range(2):
        for i in range(2):
            cross_err(4 * h + 2 * half + i, 2 * half + i).wait_recv()
        make_r(2 * h + half)
    for half in range(2):
        for i in range(2):
            gather_err(2 * half + i).wait_recv()
            cross_err(4 * (1 - h) + 2 * half + i, 4 + 2 * half + i).start()
        if half == 1:
            for i in range(2):
                pair_normed(i).start()
        for i in range(2):
            cross_err(4 * (1 - h) + 2 * half + i, 4 + 2 * half + i).wait_recv()
        make_r(2 * (1 - h) + half)
    rows_err = jnp.concatenate([err[j, share] for j in range(8)], axis=1)
    for k in range(2):
        q = c if k == 0 else 1 - c
        for n in range(4):
            cols = slice(256 * n, 256 * (n + 1))
            back = lax.dot_general(
                rows_err, fr[q, cols, :], (((1,), (1,)), ((), ())), preferred_element_type=F32
            )
            hidden = acc[q, :, cols]
            sig = jax.nn.sigmoid(hidden)
            value = (back * (sig * (1.0 + hidden * (1.0 - sig)))).astype(BF16)
            if k == 0:
                hg_ref[share, cols] = value
            else:
                hs[:, cols] = value
        if k == 0:
            pair_grad(0).start()
        else:
            cross(12).start()
    cross(12).wait()
    pair_grad(1).start()
    for i in range(4):
        gather_err(i).wait_send()
        cross_err(4 * h + i, i).wait_send()
        cross_err(4 * (1 - h) + i, 4 + i).wait_send()

    pair_normed(0).wait()
    pair_normed(1).wait()
    pair_forward().start()
    pair_forward().wait()
    for s in range(2):
        pair_grad(s).wait()

    def make_e(j, _):
        to = (z + 1 + j) % 4
        column = pl.ds(pl.multiple_of(to * 256, 256), 256)
        part = (outer(normh[l, :, column], hg_ref[...]) + outer(pn[:, column], ph[...])).astype(BF16)
        gy_e[to] = part[:, :512].reshape(4, 64, 512)
        gz_e[to] = part[:, 512:].reshape(4, 64, 512)
        for d in (1, 2, 3):
            dst = (y + d) % 4
            remote(
                gy_e.at[to, dst], r1y_e.at[d - 1, to], gs.at[13 + d], gr.at[13 + d], ydev(d)
            ).start()
        return 0

    for d in (1, 2, 3):
        lax.fori_loop(d - 1, d, make_e, 0)
        e_first_z(d).start()
    lax.fori_loop(3, 4, make_e, 0)

    for d in (1, 2, 3):
        r_first_y(d).wait()

    def add_ry(i, _):
        total = gy_r[i, :, y].astype(F32) + sum(r1y_r[d, i].astype(F32) for d in range(3))
        ay_r[i] = total.astype(BF16)
        return 0

    lax.fori_loop(0, 4, add_ry, 0)
    for d in (1, 2, 3):
        r_second_y(d).start()
    for d in (1, 2, 3):
        r_first_z(d).wait()

    def add_rz(i, _):
        total = gz_r[z, :, i].astype(F32) + sum(r1z_r[d, :, i].astype(F32) for d in range(3))
        az_r[:, i] = total.astype(BF16)
        return 0

    lax.fori_loop(0, 4, add_rz, 0)
    for d in (1, 2, 3):
        r_second_z(d).start()

    def finish_r(i):
        for d in (1, 2, 3):
            (r_second_y(d) if i == 0 else r_second_z(d)).wait()

        def own(side):
            return ay_r[z, side] if i == 0 else az_r[side, y]

        landed = r2y_r if i == 0 else r2z_r
        s_r[:, parts_r[i]] = (
            own(1 - l).astype(F32) + sum(landed[d, 1 - l].astype(F32) for d in range(3))
        ).astype(BF16)
        r_third(i).start()
        b_r[:, parts_r[i]] = own(l).astype(F32) + sum(landed[d, l].astype(F32) for d in range(3))

    for d in (1, 2, 3):
        e_first_y(d).wait()

    def add_ey(i, _):
        total = gy_e[i, y].astype(F32) + sum(r1y_e[d, i].astype(F32) for d in range(3))
        ay_e[i] = total.astype(BF16)
        return 0

    lax.fori_loop(0, 4, add_ey, 0)
    for d in (1, 2, 3):
        e_second_y(d).start()
    for d in (1, 2, 3):
        e_first_z(d).wait()

    def add_ez(i, _):
        total = gz_e[z, i].astype(F32) + sum(r1z_e[d, i].astype(F32) for d in range(3))
        az_e[i] = total.astype(BF16)
        return 0

    lax.fori_loop(0, 4, add_ez, 0)
    for d in (1, 2, 3):
        e_second_z(d).start()
    finish_r(0)
    finish_r(1)
    for i in range(2):
        for d in (1, 2, 3):
            (e_second_y(d) if i == 0 else e_second_z(d)).wait()
        mine = ay_e[z] if i == 0 else az_e[y]
        ge_ref[:, 512 * i : 512 * (i + 1)] = mine.astype(F32) + sum(r2_e[i, d].astype(F32) for d in range(3))
    for i in range(2):
        r_third(i).wait()
        gr_ref[:, parts_r[i]] = b_r[:, parts_r[i]] + r3_r[:, parts_r[i]].astype(F32)


def copy_kernel(a_in, b_in, c_in, a_out, b_out, c_out, a_mid, b_mid, c_mid, sems):
    trios = ((a_in, a_mid, a_out), (b_in, b_mid, b_out), (c_in, c_mid, c_out))
    into = [pltpu.make_async_copy(src, mid, sems.at[0, i]) for i, (src, mid, dst) in enumerate(trios)]
    out = [pltpu.make_async_copy(mid, dst, sems.at[1, i]) for i, (src, mid, dst) in enumerate(trios)]
    for copy in into:
        copy.start()
    for first, second in zip(into, out):
        first.wait()
        second.start()
    for copy in out:
        copy.wait()


def body(
    target_latents, walk_noise, step_sizes, back_gain, back_expand, back_clock, back_reduce,
    bridge_times, bridge_noise, fore_gain, fore_expand, fore_clock, fore_reduce,
):
    vmem = pl.BlockSpec(memory_space=pltpu.VMEM)
    smem = pl.BlockSpec(memory_space=pltpu.SMEM)
    hbm = pl.BlockSpec(memory_space=pl.ANY)
    dma = pltpu.SemaphoreType.DMA
    sds = jax.ShapeDtypeStruct
    R = ROWS
    outs = pl.pallas_call(
        net_kernel,
        out_shape=(sds((256, 512), F32), sds((64, 1024), F32), sds((64, 1024), F32)),
        in_specs=[vmem, hbm, smem, vmem, hbm, vmem, hbm, vmem, vmem, vmem, hbm, vmem, hbm],
        out_specs=(vmem,) * 3,
        scratch_shapes=[
            pltpu.VMEM((2, 2048, 1024), BF16), pltpu.VMEM((2, 1024, 2048), BF16),
            pltpu.VMEM((2, 2048, 1024), BF16), pltpu.VMEM((2, 1024, 2048), BF16),
            pltpu.VMEM((2, 1, 1024), F32), pltpu.VMEM((2, 1, 1024), F32),
            pltpu.VMEM((2, 4, R, 512), BF16), pltpu.VMEM((2, R, 512), BF16),
            pltpu.VMEM((8, R, 256), BF16), pltpu.VMEM((4, R, 256), F32),
            pltpu.VMEM((2, R, 1024), F32), pltpu.VMEM((2, R, 1024), BF16),
            pltpu.VMEM((4, R, 256), F32), pltpu.VMEM((4, R, 256), BF16), pltpu.VMEM((4, R, 256), BF16),
            pltpu.VMEM((4, R, 256), F32),
        ]
        + [pltpu.VMEM((4, 2, 4, 16, 384), BF16)] * 4
        + [
            pltpu.VMEM((2, 2, 2, 4, 16, 384), BF16), pltpu.VMEM((2, R, 256), F32),
            pltpu.VMEM((8, 256, 256), BF16), pltpu.VMEM((2, 256, 1024), BF16),
            pltpu.VMEM((256, 1024), BF16), pltpu.VMEM((256, 1024), BF16), pltpu.VMEM((R, 1024), BF16),
            pltpu.VMEM((256, 1024), BF16), pltpu.VMEM((256, 1024), BF16),
            pltpu.VMEM((4, 2, 4, 64, WIDE), BF16), pltpu.VMEM((4, 2, 4, 64, NARROW), BF16),
            pltpu.VMEM((3, 4, 2, 64, WIDE), BF16), pltpu.VMEM((3, 2, 4, 64, NARROW), BF16),
            pltpu.VMEM((4, 2, 64, WIDE), BF16), pltpu.VMEM((2, 4, 64, NARROW), BF16),
            pltpu.VMEM((3, 2, 64, WIDE), BF16), pltpu.VMEM((3, 2, 64, NARROW), BF16),
            pltpu.VMEM((64, 1024), F32), pltpu.VMEM((64, 1024), BF16), pltpu.VMEM((64, 1024), BF16),
            pltpu.VMEM((4, 4, 64, 512), BF16), pltpu.VMEM((4, 4, 64, 512), BF16),
            pltpu.VMEM((3, 4, 64, 512), BF16), pltpu.VMEM((3, 4, 64, 512), BF16),
            pltpu.VMEM((4, 64, 512), BF16), pltpu.VMEM((4, 64, 512), BF16),
            pltpu.VMEM((2, 3, 64, 512), BF16),
        ]
        + [dma((5,)), dma((22,)), dma((22,)), dma((12,)), dma((12,)), dma((7,)), dma((7,)), dma((31,)), dma((31,))],
        compiler_params=pltpu.CompilerParams(
            collective_id=0, has_side_effects=True, vmem_limit_bytes=62 * 2**20
        ),
        name="net",
    )(
        target_latents, walk_noise, step_sizes, back_gain.reshape(8, 1, 256), back_expand,
        back_clock.reshape(1, 1024), back_reduce, bridge_times.reshape(2, 128), bridge_noise,
        fore_gain.reshape(8, 1, 256), fore_expand, fore_clock.reshape(1, 1024), fore_reduce,
    )
    return pl.pallas_call(
        copy_kernel,
        out_shape=tuple(sds(o.shape, o.dtype) for o in outs),
        in_specs=[hbm] * 3,
        out_specs=(hbm,) * 3,
        scratch_shapes=[pltpu.VMEM(o.shape, o.dtype) for o in outs] + [dma((2, 3))],
        name="place_outputs",
    )(*outs)


def solution(mesh):
    placed = (
        P("batch", "tensor"), P(None, "batch", "tensor"), P(), P(), P(None, "tensor"), P("tensor"),
        P("tensor", None), P("batch"), P("batch", "tensor"), P(), P(None, "tensor"), P("tensor"),
        P("tensor", None),
    )
    return jax.shard_map(
        body, mesh=mesh, in_specs=placed,
        out_specs=(P("batch", "tensor"), P("batch", "tensor"), P("batch", "tensor")), check_vma=False,
    )
```

```python
import jax
import jax.numpy as jnp
from jax import lax
from jax.experimental import pallas as pl
from jax.experimental.pallas import tpu as pltpu
from jax.sharding import PartitionSpec as P

NOISE_LEVEL = 0.5
EPSILON = 1e-06
MESH = pl.DeviceIdType.MESH
F32 = jnp.float32
BF16 = jnp.bfloat16
ROWS = 128
WIDE = 640
NARROW = 384


def place():
    b = lax.axis_index("batch")
    t = lax.axis_index("tensor")
    return b // 8, (b // 4) % 2, b % 4, t // 2, t % 2


def device(z, l, y, h, c):
    return (z * 8 + l * 4 + y, h * 2 + c)


def remote(src, dst, send_sem, recv_sem, dev):
    return pltpu.make_async_remote_copy(
        src_ref=src, dst_ref=dst, send_sem=send_sem, recv_sem=recv_sem, device_id=dev, device_id_type=MESH
    )


def greet(devices):
    barrier = pltpu.get_barrier_semaphore()
    for dev in devices:
        pl.semaphore_signal(barrier, inc=1, device_id=dev, device_id_type=MESH)
    return lambda: pl.semaphore_wait(barrier, len(devices))


def batch_peers(z, l, y, h, c):
    peers = [device(z, 1 - l, y, h, c)]
    peers += [device(z, l, (y + d) % 4, h, c) for d in (1, 2, 3)]
    peers += [device((z + d) % 4, l, y, h, c) for d in (1, 2, 3)]
    return peers


def net_kernel(
    x_ref, wn_hbm, steps_ref, bg_ref, be_hbm, bc_ref, br_hbm, bt_ref, bn_ref, fg_ref, fe_hbm, fc_ref, fr_hbm,
    walk_ref, ge_ref, gr_ref,
    be, br, fe, fr, bca, fca, wn, xt, u, st, acc, ab, own, pfs, pfr, flow, m0, m1, m2, m3, mf, wx,
    err, normh, act_ref, hg_ref, hs, pn, ph,
    gy_r, gz_r, r1y_r, r1z_r, ay_r, az_r, r2y_r, r2z_r, b_r, s_r, r3_r,
    gy_e, gz_e, r1y_e, r1z_e, ay_e, az_e, r2_e,
    load_sem, cs, cr, fs, fr_sem, ms, mr, gs, gr,
):
    z, l, y, h, c = place()
    core_dev = device(z, l, y, h, 1 - c)
    far_dev = device(z, l, y, 1 - h, c)
    pair_dev = device(z, 1 - l, y, h, c)
    cut_dev = device(z, 1 - l, y, 1 - h, c)
    share = pl.ds(pl.multiple_of(c * 128, 128), 128)
    other = pl.ds(pl.multiple_of((1 - c) * 128, 128), 128)

    near_cols = pl.ds(pl.multiple_of(h * 1024, 1024), 1024)
    far_cols = pl.ds(pl.multiple_of((1 - h) * 1024, 1024), 1024)

    def load(i):
        src, dst = (
            (be_hbm, be.at[c]), (br_hbm, br.at[c]), (fe_hbm, fe.at[c]), (fr_hbm, fr.at[c]),
            (wn_hbm.at[:, share], wn.at[c]),
        )[i]
        return pltpu.make_async_copy(src, dst, load_sem.at[i])

    def cross(i):
        src, dst = (
            (be_hbm, be.at[c]), (br_hbm.at[:, far_cols], br.at[c, :, far_cols]),
            (fe_hbm, fe.at[c]), (fr_hbm, fr.at[c]),
            (wn_hbm.at[:, other], wn.at[c]),
            (x_ref.at[other], xt.at[c]),
            (bca.at[c], bca.at[c]), (fca.at[c], fca.at[c]),
            (m3.at[pl.ds(2 * (1 - c), 2)], mf.at[c]),
            (st.at[pl.ds(2 * (1 - c), 2)], wx),
            (ab.at[1 - c], act_ref.at[share]),
            (normh.at[:, share], normh.at[:, share]),
            (hs, hg_ref.at[share]),
            (br_hbm.at[:, near_cols], br.at[c, :, near_cols]),
        )[i]
        return remote(src, dst, cs.at[i], cr.at[i], core_dev)

    def cross_err(j, i):
        return remote(err.at[j, share], err.at[j, share], cs.at[14 + i], cr.at[14 + i], core_dev)

    def gather(i):
        return remote(u.at[4 * h + i], u.at[4 * h + i], fs.at[i], fr_sem.at[i], far_dev)

    def reduce(i):
        return remote(pfs.at[i], pfr.at[i], fs.at[4 + i], fr_sem.at[4 + i], far_dev)

    def gather_err(i):
        j = 4 * h + i
        return remote(err.at[j, share], err.at[j, share], fs.at[8 + i], fr_sem.at[8 + i], far_dev)

    for i in (0, 1, 4):
        load(i).start()
    arrived = greet([core_dev, far_dev, cut_dev] + batch_peers(z, l, y, h, c))
    bca[c] = bc_ref[...]
    fca[c] = fc_ref[...]
    for i in range(2):
        u[4 * h + 2 * c + i] = x_ref[share, 256 * i : 256 * (i + 1)]
    xt[c] = x_ref[share]
    arrived()
    cross(5).start()
    for i in range(2):
        gather(2 * c + i).start()
    cross(6).start()
    cross(0).start()
    cross(7).start()
    cross(5).wait()
    for i in range(2):
        u[4 * h + 2 * (1 - c) + i] = xt[1 - c, :, 256 * i : 256 * (i + 1)]
        gather(2 * (1 - c) + i).start()
    cross(1).start()
    cross(13).start()
    cross(4).start()
    for i in range(4):
        st[i] = u[4 * h + i].astype(F32)

    for s in range(2):
        noise = bn_ref[128 * s : 128 * (s + 1)].astype(F32).reshape(16, 8, 512)
        times = jnp.transpose(jnp.broadcast_to(bt_ref[s : s + 1, :], (128, 128)))
        high = times.astype(BF16).astype(F32)
        low = times - high
        packed = jnp.concatenate([noise[:, :, :256], noise[:, :, 256:]], axis=1)
        clocks = jnp.concatenate([high.reshape(16, 8, 128), low.reshape(16, 8, 128)], axis=1)
        m0[2 * s : 2 * s + 2] = (
            jnp.concatenate([packed, clocks], axis=2).astype(BF16).reshape(2, 2, 4, 16, 384)
        )

    def swap_l():
        return remote(m0.at[:, 1 - l], m1.at[:, l], ms.at[0], mr.at[0], pair_dev)

    def swap_y(d):
        to = (y + d) % 4
        return remote(m1.at[:, :, to], m2.at[:, :, y], ms.at[d], mr.at[d], device(z, l, to, h, c))

    def swap_z(d):
        to = (z + d) % 4
        return remote(m2.at[to], m3.at[z], ms.at[3 + d], mr.at[3 + d], device(to, l, y, h, c))

    swap_l().start()
    m1[:, l] = m0[:, l]

    def scaled(j, gain_ref):
        rows = u[j].astype(F32)
        return jnp.sum(rows * rows, axis=1, keepdims=True), (rows * gain_ref[j]).astype(BF16)

    def expand(gain_ref, weights, finish):
        squares = jnp.zeros((ROWS, 1), F32)
        near = []
        for i in range(4):
            square, part = scaled(4 * h + i, gain_ref)
            squares += square
            near.append(part)
        near = jnp.concatenate(near, axis=1)
        near_rows = pl.ds(pl.multiple_of(h * 1024, 1024), 1024)
        for q in range(2):
            for n in range(4):
                cols = slice(256 * n, 256 * (n + 1))
                acc[q, :, cols] = jnp.dot(near, weights[q, near_rows, cols], preferred_element_type=F32)
        for i in range(4):
            gather(i).wait_recv()
            j = 4 * (1 - h) + i
            square, part = scaled(j, gain_ref)
            squares += square
            far_rows = pl.ds(pl.multiple_of(j * 256, 256), 256)
            if i == 3:
                factor = lax.rsqrt(squares * (1.0 / 2048.0) + EPSILON)
            for q in range(2):
                for n in range(4):
                    cols = slice(256 * n, 256 * (n + 1))
                    total = acc[q, :, cols] + jnp.dot(part, weights[q, far_rows, cols], preferred_element_type=F32)
                    if i < 3:
                        acc[q, :, cols] = total
                    else:
                        finish(q, cols, total * factor)
        return factor

    def contract(weights, j):
        cols = pl.ds(pl.multiple_of(j * 256, 256), 256)
        return jnp.dot(ab[0], weights[0, :, cols], preferred_element_type=F32) + jnp.dot(
            ab[1], weights[1, :, cols], preferred_element_type=F32
        )

    def reduce_start(weights, between=lambda: None):
        for i in range(4):
            pfs[i] = contract(weights, 4 * (1 - h) + i).astype(BF16)
            reduce(i).start()
        between()
        for i in range(4):
            own[i] = contract(weights, 4 * h + i)

    def reduce_wait(i):
        reduce(i).wait()
        return own[i] + pfr[i].astype(F32)

    for i in (0, 1, 4):
        load(i).wait()
    cross(0).wait()
    cross(6).wait()
    cross(7).wait()

    def step(k, clock):
        width = steps_ref[k]

        def finish(q, cols, product):
            hidden = product + clock * bca[q, :, cols]
            ab[q, :, cols] = (hidden * jax.nn.sigmoid(hidden)).astype(BF16)

        expand(bg_ref, be, finish)

        @pl.when(k == 0)
        def _():
            cross(1).wait()

        def rest():
            @pl.when(k == 0)
            def _():
                cross(13).wait()

        reduce_start(br, rest)

        @pl.when(k == 0)
        def _():
            cross(4).wait()
            for i in (2, 3):
                load(i).start()
            cross(2).start()
            swap_l().wait()
            for d in (1, 2, 3):
                swap_y(d).start()
            m2[:, :, y] = m1[:, :, y]

        @pl.when(k == 1)
        def _():
            cross(3).start()
            for d in (1, 2, 3):
                swap_y(d).wait()
            for d in (1, 2, 3):
                swap_z(d).start()
            m3[z] = m2[z]

        @pl.when(k == 2)
        def _():
            for d in (1, 2, 3):
                swap_z(d).wait()
            cross(8).start()
            mf[c] = m3[pl.ds(2 * c, 2)]

        @pl.when(k == 3)
        def _():
            cross(8).wait()

        spread = jnp.sqrt(jnp.full((1, 256), width, F32)) * NOISE_LEVEL
        for i in range(4):
            q, cols = i // 2, slice(256 * (i % 2), 256 * (i % 2) + 256)
            state = st[i] - width * reduce_wait(i) + spread * wn[q, k, :, cols].astype(F32)
            st[i] = state
            gather(i).wait_send()

            @pl.when(k != 3)
            def _():
                u[4 * h + i] = state.astype(BF16)

            @pl.when(k == 3)
            def _():
                message = mf[q].reshape(16, 16, 384).astype(F32)
                half = slice(8 * (i % 2), 8 * (i % 2) + 8)
                noise = message[:, half, :256].reshape(ROWS, 256)
                times = (message[:, :8, 256:] + message[:, 8:, 256:]).reshape(ROWS, 128)
                times = jnp.concatenate([times] * 2, axis=1)
                start = state.astype(BF16).astype(F32)
                end = xt[q, :, cols].astype(F32)
                mixed = (1.0 - times) * start + times * end + jnp.sqrt(times * (1.0 - times)) * NOISE_LEVEL * noise
                flow[i] = (end - mixed) / (1.0 - times)
                u[4 * h + i] = mixed.astype(BF16)

            gather(i).start()
        return clock - width

    lax.fori_loop(0, 4, step, jnp.float32(1.0))

    for i in (2, 3):
        load(i).wait()
        cross(i).wait()
    cross(9).start()
    message = mf[0].reshape(16, 16, 384)[:, :, 256:].astype(F32)
    times = (message[:, :8] + message[:, 8:]).reshape(ROWS, 128)
    times = jnp.concatenate([times] * 2, axis=1)

    def finish_fore(q, cols, product):
        hidden = product + times * fca[q, :, cols]
        acc[q, :, cols] = hidden
        ab[q, :, cols] = (hidden * jax.nn.sigmoid(hidden)).astype(BF16)

    factor = expand(fg_ref, fe, finish_fore)
    reduce_start(fr)
    act_ref[share] = ab[c]
    cross(10).start()
    for j in range(8):
        normh[j % 2, share, 256 * (j // 2) : 256 * (j // 2 + 1)] = (
            u[j].astype(F32) * factor * fg_ref[j]
        ).astype(BF16)
    cross(11).start()
    cross(9).wait()
    for i in range(2):
        walk_ref[share, 256 * i : 256 * (i + 1)] = st[2 * c + i]
        walk_ref[other, 256 * i : 256 * (i + 1)] = wx[i]
    scale = 1.0 / (8192.0**0.5)
    for i in range(4):
        j = 4 * h + i
        err[j, share] = ((reduce_wait(i) - flow[i]) * scale).astype(BF16)
        gather_err(i).start()
        cross_err(j, i).start()
    for i in range(4):
        gather(i).wait_send()
    cross(10).wait()
    cross(11).wait()

    def pair_normed(i):
        part = pl.ds(pl.multiple_of(c * 128 + 64 * i, 64), 64)
        dev = pair_dev if i == 0 else cut_dev
        return remote(normh.at[1 - l, part], pn.at[part], gs.at[26 + 4 * i], gr.at[26 + 4 * i], dev)

    def ydev(d):
        return device(z, l, (y + d) % 4, h, c)

    def zdev(d):
        return device((z + d) % 4, l, y, h, c)

    def pair_forward():
        return remote(pn.at[share], pn.at[share], gs.at[27], gr.at[27], core_dev)

    def pair_grad(s):
        part = share if s == 0 else other
        return remote(hg_ref.at[part], ph.at[part], gs.at[28 + s], gr.at[28 + s], pair_dev)

    def r_first_y(d):
        return remote(gy_r.at[:, :, (y + d) % 4], r1y_r.at[d - 1], gs.at[d - 1], gr.at[d - 1], ydev(d))

    def r_first_z(d):
        return remote(gz_r.at[(z + d) % 4], r1z_r.at[d - 1], gs.at[2 + d], gr.at[2 + d], zdev(d))

    def r_second_y(d):
        return remote(ay_r.at[(z + d) % 4], r2y_r.at[d - 1], gs.at[5 + d], gr.at[5 + d], zdev(d))

    def r_second_z(d):
        return remote(az_r.at[:, (y + d) % 4], r2z_r.at[d - 1], gs.at[8 + d], gr.at[8 + d], ydev(d))

    parts_r = (slice(0, WIDE), slice(WIDE, WIDE + NARROW))

    def r_third(i):
        cols = parts_r[i]
        return remote(s_r.at[:, cols], r3_r.at[:, cols], gs.at[12 + i], gr.at[12 + i], pair_dev)

    def e_first_y(d):
        return remote(gy_e.at[:, (y + d) % 4], r1y_e.at[d - 1], gs.at[13 + d], gr.at[13 + d], ydev(d))

    def e_first_z(d):
        return remote(gz_e.at[(z + d) % 4], r1z_e.at[d - 1], gs.at[16 + d], gr.at[16 + d], zdev(d))

    def e_second_y(d):
        return remote(ay_e.at[(z + d) % 4], r2_e.at[0, d - 1], gs.at[19 + d], gr.at[19 + d], zdev(d))

    def e_second_z(d):
        return remote(az_e.at[(y + d) % 4], r2_e.at[1, d - 1], gs.at[22 + d], gr.at[22 + d], ydev(d))

    def outer(left, right):
        return lax.dot_general(left, right, (((0,), (0,)), ((), ())), preferred_element_type=F32)

    def make_r(to):
        for i in range(2):
            part = outer(err[2 * to + i], act_ref[...]).astype(BF16)
            gy_r[to, i] = part[:, :WIDE].reshape(4, 64, WIDE)
            gz_r[to, i] = part[:, WIDE:].reshape(4, 64, NARROW)
            for d in (1, 2, 3):
                dst = (y + d) % 4
                remote(
                    gy_r.at[to, i, dst], r1y_r.at[d - 1, to, i], gs.at[d - 1], gr.at[d - 1], ydev(d)
                ).start()
        for d in (1, 2, 3):

            @pl.when(to == (z + d) % 4)
            def _():
                r_first_z(d).start()

    for half in range(2):
        for i in range(2):
            cross_err(4 * h + 2 * half + i, 2 * half + i).wait_recv()
        make_r(2 * h + half)
    for half in range(2):
        for i in range(2):
            gather_err(2 * half + i).wait_recv()
            cross_err(4 * (1 - h) + 2 * half + i, 4 + 2 * half + i).start()
        if half == 1:
            for i in range(2):
                pair_normed(i).start()
        for i in range(2):
            cross_err(4 * (1 - h) + 2 * half + i, 4 + 2 * half + i).wait_recv()
        make_r(2 * (1 - h) + half)
    rows_err = jnp.concatenate([err[j, share] for j in range(8)], axis=1)
    for k in range(2):
        q = c if k == 0 else 1 - c
        for n in range(4):
            cols = slice(256 * n, 256 * (n + 1))
            back = lax.dot_general(
                rows_err, fr[q, cols, :], (((1,), (1,)), ((), ())), preferred_element_type=F32
            )
            hidden = acc[q, :, cols]
            sig = jax.nn.sigmoid(hidden)
            value = (back * (sig * (1.0 + hidden * (1.0 - sig)))).astype(BF16)
            if k == 0:
                hg_ref[share, cols] = value
            else:
                hs[:, cols] = value
        if k == 0:
            pair_grad(0).start()
        else:
            cross(12).start()
    cross(12).wait()
    pair_grad(1).start()
    for i in range(4):
        gather_err(i).wait_send()
        cross_err(4 * h + i, i).wait_send()
        cross_err(4 * (1 - h) + i, 4 + i).wait_send()

    pair_normed(0).wait()
    pair_normed(1).wait()
    pair_forward().start()
    pair_forward().wait()
    for s in range(2):
        pair_grad(s).wait()

    def make_e(j, _):
        to = (z + 1 + j) % 4
        column = pl.ds(pl.multiple_of(to * 256, 256), 256)
        part = (outer(normh[l, :, column], hg_ref[...]) + outer(pn[:, column], ph[...])).astype(BF16)
        gy_e[to] = part[:, :512].reshape(4, 64, 512)
        gz_e[to] = part[:, 512:].reshape(4, 64, 512)
        for d in (1, 2, 3):
            dst = (y + d) % 4
            remote(
                gy_e.at[to, dst], r1y_e.at[d - 1, to], gs.at[13 + d], gr.at[13 + d], ydev(d)
            ).start()
        return 0

    for d in (1, 2, 3):
        lax.fori_loop(d - 1, d, make_e, 0)
        e_first_z(d).start()
    lax.fori_loop(3, 4, make_e, 0)

    for d in (1, 2, 3):
        r_first_y(d).wait()

    def add_ry(i, _):
        total = gy_r[i, :, y].astype(F32) + sum(r1y_r[d, i].astype(F32) for d in range(3))
        ay_r[i] = total.astype(BF16)
        return 0

    lax.fori_loop(0, 4, add_ry, 0)
    for d in (1, 2, 3):
        r_second_y(d).start()
    for d in (1, 2, 3):
        r_first_z(d).wait()

    def add_rz(i, _):
        total = gz_r[z, :, i].astype(F32) + sum(r1z_r[d, :, i].astype(F32) for d in range(3))
        az_r[:, i] = total.astype(BF16)
        return 0

    lax.fori_loop(0, 4, add_rz, 0)
    for d in (1, 2, 3):
        r_second_z(d).start()

    def finish_r(i):
        for d in (1, 2, 3):
            (r_second_y(d) if i == 0 else r_second_z(d)).wait()

        def own(side):
            return ay_r[z, side] if i == 0 else az_r[side, y]

        landed = r2y_r if i == 0 else r2z_r
        s_r[:, parts_r[i]] = (
            own(1 - l).astype(F32) + sum(landed[d, 1 - l].astype(F32) for d in range(3))
        ).astype(BF16)
        r_third(i).start()
        b_r[:, parts_r[i]] = own(l).astype(F32) + sum(landed[d, l].astype(F32) for d in range(3))

    for d in (1, 2, 3):
        e_first_y(d).wait()

    def add_ey(i, _):
        total = gy_e[i, y].astype(F32) + sum(r1y_e[d, i].astype(F32) for d in range(3))
        ay_e[i] = total.astype(BF16)
        return 0

    lax.fori_loop(0, 4, add_ey, 0)
    for d in (1, 2, 3):
        e_second_y(d).start()
    for d in (1, 2, 3):
        e_first_z(d).wait()

    def add_ez(i, _):
        total = gz_e[z, i].astype(F32) + sum(r1z_e[d, i].astype(F32) for d in range(3))
        az_e[i] = total.astype(BF16)
        return 0

    lax.fori_loop(0, 4, add_ez, 0)
    for d in (1, 2, 3):
        e_second_z(d).start()
    finish_r(0)
    finish_r(1)
    for i in range(2):
        for d in (1, 2, 3):
            (e_second_y(d) if i == 0 else e_second_z(d)).wait()
        mine = ay_e[z] if i == 0 else az_e[y]
        ge_ref[:, 512 * i : 512 * (i + 1)] = mine.astype(F32) + sum(r2_e[i, d].astype(F32) for d in range(3))
    for i in range(2):
        r_third(i).wait()
        gr_ref[:, parts_r[i]] = b_r[:, parts_r[i]] + r3_r[:, parts_r[i]].astype(F32)


def copy_kernel(a_in, b_in, c_in, a_out, b_out, c_out, a_mid, b_mid, c_mid, sems):
    trios = ((a_in, a_mid, a_out), (b_in, b_mid, b_out), (c_in, c_mid, c_out))
    into, out = [], []
    for src, mid, dst in trios:
        for first in range(0, src.shape[0], 32):
            part = pl.ds(first, 32)
            into.append(pltpu.make_async_copy(src.at[part], mid.at[part], sems.at[0, len(into)]))
            out.append(pltpu.make_async_copy(mid.at[part], dst.at[part], sems.at[1, len(out)]))
    for copy in into:
        copy.start()
    for first, second in zip(into, out):
        first.wait()
        second.start()
    for copy in out:
        copy.wait()


def body(
    target_latents, walk_noise, step_sizes, back_gain, back_expand, back_clock, back_reduce,
    bridge_times, bridge_noise, fore_gain, fore_expand, fore_clock, fore_reduce,
):
    vmem = pl.BlockSpec(memory_space=pltpu.VMEM)
    smem = pl.BlockSpec(memory_space=pltpu.SMEM)
    hbm = pl.BlockSpec(memory_space=pl.ANY)
    dma = pltpu.SemaphoreType.DMA
    sds = jax.ShapeDtypeStruct
    R = ROWS
    outs = pl.pallas_call(
        net_kernel,
        out_shape=(sds((256, 512), F32), sds((64, 1024), F32), sds((64, 1024), F32)),
        in_specs=[vmem, hbm, smem, vmem, hbm, vmem, hbm, vmem, vmem, vmem, hbm, vmem, hbm],
        out_specs=(vmem,) * 3,
        scratch_shapes=[
            pltpu.VMEM((2, 2048, 1024), BF16), pltpu.VMEM((2, 1024, 2048), BF16),
            pltpu.VMEM((2, 2048, 1024), BF16), pltpu.VMEM((2, 1024, 2048), BF16),
            pltpu.VMEM((2, 1, 1024), F32), pltpu.VMEM((2, 1, 1024), F32),
            pltpu.VMEM((2, 4, R, 512), BF16), pltpu.VMEM((2, R, 512), BF16),
            pltpu.VMEM((8, R, 256), BF16), pltpu.VMEM((4, R, 256), F32),
            pltpu.VMEM((2, R, 1024), F32), pltpu.VMEM((2, R, 1024), BF16),
            pltpu.VMEM((4, R, 256), F32), pltpu.VMEM((4, R, 256), BF16), pltpu.VMEM((4, R, 256), BF16),
            pltpu.VMEM((4, R, 256), F32),
        ]
        + [pltpu.VMEM((4, 2, 4, 16, 384), BF16)] * 4
        + [
            pltpu.VMEM((2, 2, 2, 4, 16, 384), BF16), pltpu.VMEM((2, R, 256), F32),
            pltpu.VMEM((8, 256, 256), BF16), pltpu.VMEM((2, 256, 1024), BF16),
            pltpu.VMEM((256, 1024), BF16), pltpu.VMEM((256, 1024), BF16), pltpu.VMEM((R, 1024), BF16),
            pltpu.VMEM((256, 1024), BF16), pltpu.VMEM((256, 1024), BF16),
            pltpu.VMEM((4, 2, 4, 64, WIDE), BF16), pltpu.VMEM((4, 2, 4, 64, NARROW), BF16),
            pltpu.VMEM((3, 4, 2, 64, WIDE), BF16), pltpu.VMEM((3, 2, 4, 64, NARROW), BF16),
            pltpu.VMEM((4, 2, 64, WIDE), BF16), pltpu.VMEM((2, 4, 64, NARROW), BF16),
            pltpu.VMEM((3, 2, 64, WIDE), BF16), pltpu.VMEM((3, 2, 64, NARROW), BF16),
            pltpu.VMEM((64, 1024), F32), pltpu.VMEM((64, 1024), BF16), pltpu.VMEM((64, 1024), BF16),
            pltpu.VMEM((4, 4, 64, 512), BF16), pltpu.VMEM((4, 4, 64, 512), BF16),
            pltpu.VMEM((3, 4, 64, 512), BF16), pltpu.VMEM((3, 4, 64, 512), BF16),
            pltpu.VMEM((4, 64, 512), BF16), pltpu.VMEM((4, 64, 512), BF16),
            pltpu.VMEM((2, 3, 64, 512), BF16),
        ]
        + [dma((5,)), dma((22,)), dma((22,)), dma((12,)), dma((12,)), dma((7,)), dma((7,)), dma((31,)), dma((31,))],
        compiler_params=pltpu.CompilerParams(
            collective_id=0, has_side_effects=True, vmem_limit_bytes=62 * 2**20
        ),
        name="net",
    )(
        target_latents, walk_noise, step_sizes, back_gain.reshape(8, 1, 256), back_expand,
        back_clock.reshape(1, 1024), back_reduce, bridge_times.reshape(2, 128), bridge_noise,
        fore_gain.reshape(8, 1, 256), fore_expand, fore_clock.reshape(1, 1024), fore_reduce,
    )
    return pl.pallas_call(
        copy_kernel,
        out_shape=tuple(sds(o.shape, o.dtype) for o in outs),
        in_specs=[hbm] * 3,
        out_specs=(hbm,) * 3,
        scratch_shapes=[pltpu.VMEM(o.shape, o.dtype) for o in outs] + [dma((2, 12))],
        name="place_outputs",
    )(*outs)


def solution(mesh):
    placed = (
        P("batch", "tensor"), P(None, "batch", "tensor"), P(), P(), P(None, "tensor"), P("tensor"),
        P("tensor", None), P("batch"), P("batch", "tensor"), P(), P(None, "tensor"), P("tensor"),
        P("tensor", None),
    )
    return jax.shard_map(
        body, mesh=mesh, in_specs=placed,
        out_specs=(P("batch", "tensor"), P("batch", "tensor"), P("batch", "tensor")), check_vma=False,
    )
```
